32 devices in a mesh: prow: 4 (over y, x), pcol: 8 (over z, core).
Axes of the slice: x: 2, y: 2, z: 4, core: 2. Of those that a mesh axis runs over, the one named last changes fastest.
Arguments:
- adjoint_trail: float32 [8, 4, 256, 4, 8, 256], P(None, 'prow', None, None, 'pcol'), as said below
- factor_low: float32 [8, 4, 8, 32, 4, 256], P(None, 'prow', 'pcol'), may hold values from -0.0625 to 0.0625
- adjoint_low: float32 [8, 4, 8, 32, 4, 256], P(None, 'prow', 'pcol'), may hold values from -6 to 6
- factor_top: float32 [10, 256, 256], P(None, 'pcol'), as said below
- adjoint_top: float32 [10, 256, 256], P(None, 'pcol'), may hold values from -6 to 6
- diag_inverse: float32 [4, 256, 256], P(None, 'pcol'), as said below
Outputs:
- grad_low: float32 [8, 4, 8, 32, 4, 256], P(None, 'prow', 'pcol')
- grad_top: float32 [10, 256, 256], P(None, 'pcol')
The draws below stay inside these ranges and needn't reach their ends.
Inputs may be any that keep to these rules, and one draw needn't show every extreme that they name: adjoint_trail reshaped row-major to 8192 x 8192 is symmetric. The diagonal blocks factor_top[j (j + 1) / 2 + j] are lower triangular with a positive diagonal. diag_inverse[j] is the inverse of factor_top[j (j + 1) / 2 + j].
All inputs are finite; a program needn't handle non-finite values.
Results may differ from the reference program's by a relative error of at most 0.00024.
Values sent between devices are 32-bit elements; how exact they have to be, the bound alone decides.
No kernel may reach another device: no remote copies, remote signals or barrier semaphores. Data moves between devices by JAX's collectives and lax.ppermute only.
A program may use at most 128 MiB of HBM per device.

```python
import math
import jax
import jax.numpy as jnp
from jax import lax

NB = 256
K = 4
M = 8192
NBLK = 10
MROW = 8
MCOL = 4
RSUB = 32
N_PROW = 4
N_PCOL = 8


def draw_adjoint_trail(key, part):
    first = jax.random.fold_in(key, 0)
    raw = jax.random.normal(first, (M, M), jnp.float32)
    symmetric = (raw + raw.T) * 0.7071
    return symmetric.reshape(MROW, N_PROW, NB, MCOL, N_PCOL, NB)


def diagonal_blocks(key):
    first, second = jax.random.split(jax.random.fold_in(key, 11))
    pivots = jnp.exp(jax.random.uniform(first, (K, NB), jnp.float32, math.log(0.7), math.log(1.4)))
    below = jax.random.normal(second, (K, NB, NB), jnp.float32) * (0.4 / math.sqrt(NB))
    row_ids = lax.broadcasted_iota(jnp.int32, (K, NB, NB), 1)
    col_ids = lax.broadcasted_iota(jnp.int32, (K, NB, NB), 2)
    strict = jnp.where(row_ids > col_ids, below, 0.0)
    return strict + jnp.where(row_ids == col_ids, pivots[:, :, None], 0.0)


def draw_factor_top(key, part):
    blocks = diagonal_blocks(key)
    noise = jax.random.normal(jax.random.fold_in(key, 12), (NBLK, NB, NB), jnp.float32) * (1.0 / math.sqrt(NB))
    for panel in range(K):
        noise = noise.at[panel * (panel + 1) // 2 + panel].set(blocks[panel])
    return noise


def invert_lower(block):
    identity = jnp.eye(NB, dtype=jnp.float32)
    return jax.scipy.linalg.solve_triangular(block, identity, lower=True)


def draw_diag_inverse(key, part):
    return jax.vmap(invert_lower)(diagonal_blocks(key))


def steps_of(own_key, dims, cuts, least, high):
    def one(axis_at, parts):
        draws = jax.random.uniform(jax.random.fold_in(jax.random.fold_in(own_key, 6), axis_at), (parts,), jnp.float32, least / len(cuts), high / len(cuts))
        return jnp.repeat(jnp.exp(draws), dims[axis_at] // parts).reshape((-1,) + (1,) * (len(dims) - axis_at - 1))

    loudness = one(*cuts[0])
    for cut in cuts[1:]:
        loudness = loudness * one(*cut)
    return loudness


def bell_draw(own_key, shape, deviation, most, shards=(), held_as=jnp.bfloat16):
    level = steps_of(own_key, shape, shards, -0.22, 0.18) if shards else 1.0
    values = jax.random.normal(own_key, shape, jnp.float32) * deviation * level
    return jnp.minimum(jnp.maximum(values, -most), most).astype(held_as)


def setup_inputs(seed: int = 0) -> dict:
    streams_of = jax.random.split(jax.random.key(seed), 7)
    return {
        "adjoint_trail": draw_adjoint_trail(jax.random.fold_in(streams_of[6], 71), 0),
        "factor_low": bell_draw(streams_of[1], (MROW, N_PROW, N_PCOL, RSUB, K, NB), M ** -0.5, 0.0625, ((1, 4), (2, 8)), jnp.float32),
        "adjoint_low": bell_draw(streams_of[2], (MROW, N_PROW, N_PCOL, RSUB, K, NB), 1.0, 6.0, ((1, 4), (2, 8)), jnp.float32),
        "factor_top": draw_factor_top(jax.random.fold_in(streams_of[6], 71), 0),
        "adjoint_top": bell_draw(streams_of[4], (NBLK, NB, NB), 1.0, 6.0, ((1, 8),), jnp.float32),
        "diag_inverse": draw_diag_inverse(jax.random.fold_in(streams_of[6], 71), 0),
    }


HIGHEST = lax.Precision.HIGHEST

def matmul(left, right):
    return jnp.dot(left.astype(jnp.float32), right.astype(jnp.float32), precision=HIGHEST, preferred_element_type=jnp.float32)

def half_lower(square):
    size = square.shape[0]
    row_ids = lax.broadcasted_iota(jnp.int32, (size, size), 0)
    col_ids = lax.broadcasted_iota(jnp.int32, (size, size), 1)
    return jnp.where(row_ids > col_ids, square, jnp.where(row_ids == col_ids, 0.5 * square, 0.0))

def assemble(top_blocks, low_part):
    span = K * NB
    upper = jnp.zeros((span, span), jnp.float32)
    for row_block in range(K):
        for col_block in range(row_block + 1):
            piece = top_blocks[row_block * (row_block + 1) // 2 + col_block]
            if row_block == col_block:
                piece = jnp.tril(piece)
            upper = upper.at[row_block * NB:(row_block + 1) * NB, col_block * NB:(col_block + 1) * NB].set(piece)
    return jnp.concatenate([upper, low_part.reshape(M, span)], axis=0)

def reference(adjoint_trail, factor_low, adjoint_low, factor_top, adjoint_top, diag_inverse):
    span = K * NB
    order = span + M
    factor = assemble(factor_top, factor_low)
    adjoint = assemble(adjoint_top, adjoint_low)
    collected = jnp.zeros((order, order), jnp.float32).at[span:, span:].set(adjoint_trail.reshape(M, M))
    gradients = [None] * K
    diagonals = [None] * K
    for panel in reversed(range(K)):
        low = panel * NB
        high = low + NB
        columns = factor[high:, low:high]
        diagonal = factor[low:high, low:high]
        residual = adjoint[high:, low:high] - 2.0 * matmul(collected[high:, high:], columns)
        gradient = matmul(residual, diag_inverse[panel])
        lower_adj = jnp.tril(adjoint[low:high, low:high] - matmul(gradient.T, columns))
        inner = half_lower(matmul(diagonal.T, lower_adj))
        spread = matmul(diag_inverse[panel].T, matmul(inner, diag_inverse[panel]))
        diag_grad = 0.5 * (spread + spread.T)
        collected = collected.at[high:, low:high].set(0.5 * gradient)
        collected = collected.at[low:high, high:].set(0.5 * gradient.T)
        collected = collected.at[low:high, low:high].set(diag_grad)
        gradients[panel] = gradient
        diagonals[panel] = diag_grad
    grad_low = jnp.stack([gradients[p][span - (p + 1) * NB:] for p in range(K)], 1).reshape(factor_low.shape)
    blocks = []
    for row_block in range(K):
        for col_block in range(row_block + 1):
            if row_block == col_block:
                blocks.append(diagonals[col_block])
            else:
                offset = (row_block - col_block - 1) * NB
                blocks.append(gradients[col_block][offset:offset + NB])
    grad_top = jnp.stack(blocks)
    return (grad_low, grad_top)
```

```python
import jax
import jax.numpy as jnp
from jax import lax
from jax.sharding import PartitionSpec as P

NB = 256
K = 4


HIGHEST = lax.Precision.HIGHEST


def from_root(array, axis, root):
    mine = lax.axis_index(axis) == root
    return lax.psum(jnp.where(mine, array, jnp.zeros_like(array)), axis)


def matmul(left, right):
    return jnp.dot(left, right, precision=HIGHEST, preferred_element_type=jnp.float32)


def inner_product(left, right):
    return lax.dot_general(
        left, right, (((0,), (0,)), ((), ())), precision=HIGHEST, preferred_element_type=jnp.float32
    )


def block_slot(row_block, col_block):
    return row_block * (row_block + 1) // 2 + col_block


def half_lower(square):
    size = square.shape[0]
    row_ids = lax.broadcasted_iota(jnp.int32, (size, size), 0)
    col_ids = lax.broadcasted_iota(jnp.int32, (size, size), 1)
    return jnp.where(row_ids > col_ids, square, jnp.where(row_ids == col_ids, 0.5 * square, 0.0))


def diagonal_adjoint(diagonal, inverse, lower_adj):
    inner = half_lower(inner_product(jnp.tril(diagonal), lower_adj))
    spread = inner_product(inverse, matmul(inner, inverse))
    return 0.5 * (spread + spread.T)


def rows_one(piece):
    return lax.all_gather(piece, "pcol", axis=1, tiled=True)


def owner_one(piece, root):
    return from_root(piece, "prow", root)


def reduce_one(term, count):
    return lax.psum_scatter(
        term(jnp.int32(0), lax.axis_size("pcol") * count), "pcol", scatter_dimension=0, tiled=True
    )


def trailing_product(trail, panels, gather_rows, send_owner, reduce_rows):
    prow_count = lax.axis_size("prow")
    pcol_count = lax.axis_size("pcol")
    cycles, sub_rows, width = panels.shape
    block = sub_rows * pcol_count
    gathered = gather_rows(panels[:, None]).reshape(cycles, block, width)
    column = lax.axis_index("pcol")
    col_cycles = trail.shape[3]
    owned = []
    for cycle in range(col_cycles):
        global_block = cycle * pcol_count + column
        share = lax.dynamic_index_in_dim(gathered, global_block // prow_count, 0, keepdims=False)
        owned.append(send_owner(share, global_block % prow_count))
    stacked = jnp.stack(owned)
    view = trail.reshape(cycles, pcol_count, sub_rows, col_cycles, block)
    unit = cycles * sub_rows

    def term(start, count):
        product = jnp.einsum(
            "iaekb,kbn->aien", view, stacked, precision=HIGHEST, preferred_element_type=jnp.float32
        )
        return product.reshape(count, width)

    return reduce_rows(term, unit).reshape(cycles, sub_rows, width)


def per_device_any(adjoint_trail, factor_low, adjoint_low, factor_top, adjoint_top, diag_inverse):
    cycles = factor_low.shape[0]
    sub_rows = factor_low.shape[3]
    local_rows = cycles * sub_rows
    low_factor = factor_low.reshape(cycles, sub_rows, K * NB)
    low_adjoint = adjoint_low.reshape(local_rows, K, NB)
    columns = low_factor.reshape(local_rows, K, NB)
    top_factor, top_adjoint, inverses = (
        lax.all_gather(factor_top, "pcol", axis=1, tiled=True),
        lax.all_gather(adjoint_top, "pcol", axis=1, tiled=True),
        lax.all_gather(diag_inverse, "pcol", axis=1, tiled=True),
    )
    lower_grads = [None] * K
    diag_grads = [None] * K
    upper_grads = {}
    grams = {}

    def lower_step(panel):
        single = low_factor[:, :, panel * NB : (panel + 1) * NB]
        image = trailing_product(adjoint_trail, single, rows_one, owner_one, reduce_one).reshape(
            local_rows, NB
        )
        residual = low_adjoint[:, panel] - 2.0 * image
        for later in range(panel + 1, K):
            residual = residual - matmul(lower_grads[later], top_factor[block_slot(later, panel)])
        lower_grads[panel] = matmul(residual, inverses[panel])

    def top_step(panel):
        for row_block in range(panel + 1, K):
            top_residual = top_adjoint[block_slot(row_block, panel)] - grams[row_block, panel]
            top_residual = top_residual - 2.0 * matmul(
                diag_grads[row_block], top_factor[block_slot(row_block, panel)]
            )
            for middle in range(panel + 1, row_block):
                top_residual = top_residual - matmul(
                    upper_grads[middle, row_block], top_factor[block_slot(middle, panel)]
                )
            for beyond in range(row_block + 1, K):
                top_residual = top_residual - inner_product(
                    upper_grads[row_block, beyond], top_factor[block_slot(beyond, panel)]
                )
            upper_grads[panel, row_block] = matmul(top_residual, inverses[panel])
        lower_adj = top_adjoint[block_slot(panel, panel)] - grams[panel, panel]
        for row_block in range(panel + 1, K):
            lower_adj = lower_adj - inner_product(
                upper_grads[panel, row_block], top_factor[block_slot(row_block, panel)]
            )
        diag_grads[panel] = diagonal_adjoint(
            top_factor[block_slot(panel, panel)], inverses[panel], jnp.tril(lower_adj)
        )

    for panel in reversed(range(K)):
        lower_step(panel)
        local_gram = jnp.stack(
            [inner_product(lower_grads[panel], columns[:, earlier]) for earlier in range(panel + 1)]
        )
        summed = lax.psum(local_gram, ("prow", "pcol"))
        for earlier in range(panel + 1):
            grams[panel, earlier] = summed[earlier]
        top_step(panel)
    grad_low = jnp.stack(lower_grads, 1).reshape(factor_low.shape)
    blocks = []
    for row_block in range(K):
        for col_block in range(row_block + 1):
            if row_block == col_block:
                blocks.append(diag_grads[col_block])
            else:
                blocks.append(upper_grads[col_block, row_block])
    full_top = jnp.stack(blocks)
    share_rows = factor_top.shape[1]
    grad_top = lax.dynamic_slice_in_dim(
        full_top, lax.axis_index("pcol") * share_rows, share_rows, 1
    )
    return (grad_low, grad_top)


AXES = ("prow", "pcol")
NZ = 4
HIGH = lax.Precision.HIGH
HOLDS = ((0, 2, 1, 3), (1, 3, 0, 2), (2, 0, 3, 1), (3, 1, 2, 0))


def route(place):
    pairs = []
    for prow in range(4):
        for pcol in range(8):
            goal = place(prow, pcol // 2, pcol % 2)
            if goal is not None:
                pairs.append((prow * 8 + pcol, goal[0] * 8 + goal[1] * 2 + goal[2]))
    return pairs


CORE = route(lambda p, z, c: (p, z, 1 - c))
UP = route(lambda p, z, c: (p, z + 1, c) if z + 1 < NZ else None)
DOWN = route(lambda p, z, c: (p, z - 1, c) if z > 0 else None)
PLANE = {d: route(lambda p, z, c, d=d: (p ^ d, z, c)) for d in (1, 2, 3)}
LINE = {d: route(lambda p, z, c, d=d: (p, z ^ d, c)) for d in (1, 2, 3)}
HOME = {
    s: route(lambda p, z, c, s=s: ((z % 2) * 2 + c, HOLDS[p][z], (z // 2) ^ s)) for s in (0, 1)
}


def move(array, pairs):
    return lax.ppermute(array, AXES, pairs)


def mm(left, right, dims=((1,), (0,))):
    return lax.dot_general(
        left, right, (dims, ((), ())), precision=HIGH, preferred_element_type=jnp.float32
    )


def line_gather(piece):
    up, down = [piece], [piece]
    for _ in range(NZ - 1):
        up.append(move(up[-1], UP))
        down.append(move(down[-1], DOWN))
    return jnp.stack([down[t] + up[NZ - t] for t in range(1, NZ)])


def pick(array, index, axis):
    return lax.dynamic_index_in_dim(array, index, axis, keepdims=False)


def per_device(adjoint_trail, factor_low, adjoint_low, factor_top, adjoint_top, diag_inverse):
    cycles, sub_rows = factor_low.shape[0], factor_low.shape[3]
    col_cycles = adjoint_trail.shape[3]
    local_rows = cycles * sub_rows
    prow, pcol = lax.axis_index("prow"), lax.axis_index("pcol")
    layer, core = pcol // 2, pcol % 2
    holds = jnp.array(HOLDS, jnp.int32)
    columns = factor_low.reshape(local_rows, K * NB)
    low_adjoint = adjoint_low.reshape(local_rows, K, NB)

    trail = adjoint_trail.reshape(cycles, NZ, 2, sub_rows, col_cycles * NB)
    trail = lax.dynamic_slice_in_dim(jnp.concatenate([trail, trail], 1), layer, NZ, 1)
    trail = jnp.where(core == 0, trail, trail[:, :, ::-1])
    trail = trail.transpose(4, 2, 1, 0, 3).reshape(col_cycles * NB, -1)

    def image(panel):
        piece = factor_low[:, 0, 0, :, panel]
        others = line_gather(piece)
        whole = jnp.concatenate(
            [piece[None], others, move(piece, CORE)[None], move(others, CORE)]
        ).reshape(-1, NB)
        partial = mm(trail, whole).reshape(col_cycles, NZ, 2 * sub_rows, NB)
        total = pick(partial, holds[prow, layer], 1)
        for d in (1, 2, 3):
            total = total + move(pick(partial, holds[prow ^ d, layer], 1), PLANE[d])
        total = total.reshape(col_cycles, 2, sub_rows, NB)
        same = move(pick(total, layer // 2, 1), HOME[0])
        cross = move(pick(total, 1 - layer // 2, 1), HOME[1])
        even = jnp.where(core == 0, same, cross)
        odd = jnp.where(core == 0, cross, same)
        return jnp.stack([even, odd], 1).reshape(local_rows, NB)

    def gather_top(local):
        blocks, rows = local.shape[0], local.shape[1]
        share = rows // 4
        mine = pick(local.reshape(blocks, 4, share, NB), prow, 1)
        others = line_gather(mine)
        lines = jnp.concatenate([mine[None], others])
        planes = jnp.stack([lines] + [move(lines, PLANE[d]) for d in (1, 2, 3)])
        cores = jnp.stack([planes, move(planes, CORE)])
        z_order = (jnp.arange(NZ) - layer) % NZ
        cores = cores[jnp.arange(2) ^ core][:, jnp.arange(4) ^ prow][:, :, z_order]
        return cores.transpose(3, 2, 0, 1, 4, 5).reshape(blocks, -1, NB)

    top = gather_top(jnp.concatenate([factor_top, diag_inverse]))
    count = factor_top.shape[0]
    top_factor, inverses = top[:count], top[count:]

    own_top = jnp.where(prow == 0, adjoint_top, jnp.zeros_like(adjoint_top))
    share_rows = factor_top.shape[1]
    term_top = lax.dynamic_update_slice_in_dim(
        jnp.zeros((count, NB, NB), jnp.float32), own_top, pcol * share_rows, 1
    )

    lower, upper, diag, grams = [None] * K, {}, [None] * K, {}

    def lower_step(panel):
        residual = low_adjoint[:, panel] - 2.0 * image(panel)
        for later in range(panel + 1, K):
            residual = residual - mm(lower[later], top_factor[block_slot(later, panel)])
        lower[panel] = mm(residual, inverses[panel])
        gram = mm(lower[panel], columns[:, : (panel + 1) * NB], ((0,), (0,)))
        for earlier in range(panel + 1):
            grams[panel, earlier] = gram[:, earlier * NB : (earlier + 1) * NB]

    def off_diagonal(panel):
        for row in range(panel + 1, K):
            total = term_top[block_slot(row, panel)] - grams[row, panel]
            total = total - 2.0 * mm(diag[row], top_factor[block_slot(row, panel)])
            for middle in range(panel + 1, row):
                total = total - mm(upper[middle, row], top_factor[block_slot(middle, panel)])
            for beyond in range(row + 1, K):
                total = total - mm(
                    upper[row, beyond], top_factor[block_slot(beyond, panel)], ((0,), (0,))
                )
            upper[panel, row] = mm(total, inverses[panel])

    def on_diagonal(panel):
        total = term_top[block_slot(panel, panel)] - grams[panel, panel]
        for row in range(panel + 1, K):
            total = total - mm(upper[panel, row], top_factor[block_slot(row, panel)], ((0,), (0,)))
        factor = jnp.tril(top_factor[block_slot(panel, panel)])
        inner = half_lower(mm(factor, jnp.tril(total), ((0,), (0,))))
        spread = mm(inverses[panel], mm(inner, inverses[panel]), ((0,), (0,)))
        diag[panel] = 0.5 * (spread + spread.T)

    def scatter_top(blocks):
        parts = blocks.reshape(-1, NZ, 2, share_rows, NB)
        total = pick(parts, core, 2) + move(pick(parts, 1 - core, 2), CORE)
        kept = pick(total, layer, 1)
        for d in (1, 2, 3):
            kept = kept + move(pick(total, layer ^ d, 1), LINE[d])
        return kept + sum(move(kept, PLANE[d]) for d in (1, 2, 3))

    for panel in reversed(range(K)):
        off_diagonal(panel)
        lower_step(panel)
        on_diagonal(panel)
    early = {}
    order = []
    for panel in reversed(range(K)):
        group = [(row, panel) for row in range(panel + 1, K)] + [(panel, panel)]
        if panel == 0:
            order.append(group[:-1])
            order.append(group[-1:])
        else:
            order.append(group)
    for group in order:
        stacked = jnp.stack([diag[c] if r == c else upper[c, r] for r, c in group])
        summed = scatter_top(stacked)
        for at, key in enumerate(group):
            early[key] = summed[at]
    grad_low = jnp.stack(lower, 1).reshape(factor_low.shape)
    grad_top = jnp.stack([early[r, c] for r in range(K) for c in range(r + 1)])
    return (grad_low, grad_top)


def covers(mesh):
    return mesh.shape["prow"] == 4 and mesh.shape["pcol"] == 8


def solution(mesh):
    in_specs = (
        P(None, "prow", None, None, "pcol", None),
        P(None, "prow", "pcol", None, None, None),
        P(None, "prow", "pcol", None, None, None),
        P(None, "pcol", None),
        P(None, "pcol", None),
        P(None, "pcol", None),
    )
    out_specs = (P(None, "prow", "pcol", None, None, None), P(None, "pcol", None))
    return jax.shard_map(
        per_device if covers(mesh) else per_device_any, mesh=mesh, in_specs=in_specs, out_specs=out_specs, check_vma=False
    )
```

```python
import jax
import jax.numpy as jnp
from jax import lax
from jax.experimental import pallas as pl
from jax.experimental.pallas import tpu as pltpu
from jax.sharding import PartitionSpec as P

NB = 256
K = 4


HIGHEST = lax.Precision.HIGHEST


def from_root(array, axis, root):
    mine = lax.axis_index(axis) == root
    return lax.psum(jnp.where(mine, array, jnp.zeros_like(array)), axis)


def matmul(left, right):
    return jnp.dot(left, right, precision=HIGHEST, preferred_element_type=jnp.float32)


def inner_product(left, right):
    return lax.dot_general(
        left, right, (((0,), (0,)), ((), ())), precision=HIGHEST, preferred_element_type=jnp.float32
    )


def block_slot(row_block, col_block):
    return row_block * (row_block + 1) // 2 + col_block


def half_lower(square):
    size = square.shape[0]
    row_ids = lax.broadcasted_iota(jnp.int32, (size, size), 0)
    col_ids = lax.broadcasted_iota(jnp.int32, (size, size), 1)
    return jnp.where(row_ids > col_ids, square, jnp.where(row_ids == col_ids, 0.5 * square, 0.0))


def diagonal_adjoint(diagonal, inverse, lower_adj):
    inner = half_lower(inner_product(jnp.tril(diagonal), lower_adj))
    spread = inner_product(inverse, matmul(inner, inverse))
    return 0.5 * (spread + spread.T)


def rows_one(piece):
    return lax.all_gather(piece, "pcol", axis=1, tiled=True)


def owner_one(piece, root):
    return from_root(piece, "prow", root)


def reduce_one(term, count):
    return lax.psum_scatter(
        term(jnp.int32(0), lax.axis_size("pcol") * count), "pcol", scatter_dimension=0, tiled=True
    )


def trailing_product(trail, panels, gather_rows, send_owner, reduce_rows):
    prow_count = lax.axis_size("prow")
    pcol_count = lax.axis_size("pcol")
    cycles, sub_rows, width = panels.shape
    block = sub_rows * pcol_count
    gathered = gather_rows(panels[:, None]).reshape(cycles, block, width)
    column = lax.axis_index("pcol")
    col_cycles = trail.shape[3]
    owned = []
    for cycle in range(col_cycles):
        global_block = cycle * pcol_count + column
        share = lax.dynamic_index_in_dim(gathered, global_block // prow_count, 0, keepdims=False)
        owned.append(send_owner(share, global_block % prow_count))
    stacked = jnp.stack(owned)
    view = trail.reshape(cycles, pcol_count, sub_rows, col_cycles, block)
    unit = cycles * sub_rows

    def term(start, count):
        product = jnp.einsum(
            "iaekb,kbn->aien", view, stacked, precision=HIGHEST, preferred_element_type=jnp.float32
        )
        return product.reshape(count, width)

    return reduce_rows(term, unit).reshape(cycles, sub_rows, width)


def per_device_any(adjoint_trail, factor_low, adjoint_low, factor_top, adjoint_top, diag_inverse):
    cycles = factor_low.shape[0]
    sub_rows = factor_low.shape[3]
    local_rows = cycles * sub_rows
    low_factor = factor_low.reshape(cycles, sub_rows, K * NB)
    low_adjoint = adjoint_low.reshape(local_rows, K, NB)
    columns = low_factor.reshape(local_rows, K, NB)
    top_factor, top_adjoint, inverses = (
        lax.all_gather(factor_top, "pcol", axis=1, tiled=True),
        lax.all_gather(adjoint_top, "pcol", axis=1, tiled=True),
        lax.all_gather(diag_inverse, "pcol", axis=1, tiled=True),
    )
    lower_grads = [None] * K
    diag_grads = [None] * K
    upper_grads = {}
    grams = {}

    def lower_step(panel):
        single = low_factor[:, :, panel * NB : (panel + 1) * NB]
        image = trailing_product(adjoint_trail, single, rows_one, owner_one, reduce_one).reshape(
            local_rows, NB
        )
        residual = low_adjoint[:, panel] - 2.0 * image
        for later in range(panel + 1, K):
            residual = residual - matmul(lower_grads[later], top_factor[block_slot(later, panel)])
        lower_grads[panel] = matmul(residual, inverses[panel])

    def top_step(panel):
        for row_block in range(panel + 1, K):
            top_residual = top_adjoint[block_slot(row_block, panel)] - grams[row_block, panel]
            top_residual = top_residual - 2.0 * matmul(
                diag_grads[row_block], top_factor[block_slot(row_block, panel)]
            )
            for middle in range(panel + 1, row_block):
                top_residual = top_residual - matmul(
                    upper_grads[middle, row_block], top_factor[block_slot(middle, panel)]
                )
            for beyond in range(row_block + 1, K):
                top_residual = top_residual - inner_product(
                    upper_grads[row_block, beyond], top_factor[block_slot(beyond, panel)]
                )
            upper_grads[panel, row_block] = matmul(top_residual, inverses[panel])
        lower_adj = top_adjoint[block_slot(panel, panel)] - grams[panel, panel]
        for row_block in range(panel + 1, K):
            lower_adj = lower_adj - inner_product(
                upper_grads[panel, row_block], top_factor[block_slot(row_block, panel)]
            )
        diag_grads[panel] = diagonal_adjoint(
            top_factor[block_slot(panel, panel)], inverses[panel], jnp.tril(lower_adj)
        )

    for panel in reversed(range(K)):
        lower_step(panel)
        local_gram = jnp.stack(
            [inner_product(lower_grads[panel], columns[:, earlier]) for earlier in range(panel + 1)]
        )
        summed = lax.psum(local_gram, ("prow", "pcol"))
        for earlier in range(panel + 1):
            grams[panel, earlier] = summed[earlier]
        top_step(panel)
    grad_low = jnp.stack(lower_grads, 1).reshape(factor_low.shape)
    blocks = []
    for row_block in range(K):
        for col_block in range(row_block + 1):
            if row_block == col_block:
                blocks.append(diag_grads[col_block])
            else:
                blocks.append(upper_grads[col_block, row_block])
    full_top = jnp.stack(blocks)
    share_rows = factor_top.shape[1]
    grad_top = lax.dynamic_slice_in_dim(
        full_top, lax.axis_index("pcol") * share_rows, share_rows, 1
    )
    return (grad_low, grad_top)


AXES = ("prow", "pcol")
NZ = 4
LANES = 128
VMEM = 48 * 1024 * 1024
GROUPS = ((3, 2), (1, 0))
HOLDS = ((0, 2, 1, 3), (1, 3, 0, 2), (2, 0, 3, 1), (3, 1, 2, 0))


def route(place):
    pairs = []
    for prow in range(4):
        for pcol in range(8):
            goal = place(prow, pcol // 2, pcol % 2)
            if goal is not None:
                pairs.append((prow * 8 + pcol, goal[0] * 8 + goal[1] * 2 + goal[2]))
    return pairs


CORE = route(lambda p, z, c: (p, z, 1 - c))
UP = route(lambda p, z, c: (p, z + 1, c) if z + 1 < NZ else None)
DOWN = route(lambda p, z, c: (p, z - 1, c) if z > 0 else None)
PLANE = {d: route(lambda p, z, c, d=d: (p ^ d, z, c)) for d in (1, 2, 3)}
LINE = {d: route(lambda p, z, c, d=d: (p, z ^ d, c)) for d in (1, 2, 3)}
HOME = {
    s: route(lambda p, z, c, s=s: ((z % 2) * 2 + c, HOLDS[p][z], (z // 2) ^ s)) for s in (0, 1)
}


def move(array, pairs):
    return lax.ppermute(array, AXES, pairs)


def pick(array, index, axis):
    return lax.dynamic_index_in_dim(array, index, axis, keepdims=False)


def call(body, out, cost, **more):
    flops, bytes_accessed = cost
    return pl.pallas_call(
        body,
        out_shape=out,
        compiler_params=pltpu.CompilerParams(vmem_limit_bytes=VMEM),
        cost_estimate=pl.CostEstimate(
            flops=flops, bytes_accessed=bytes_accessed, transcendentals=0
        ),
        **more,
    )


def struct(*shape, dtype=jnp.float32):
    return jax.ShapeDtypeStruct(shape, dtype)


def split(value):
    high = value.astype(jnp.bfloat16)
    return high, (value - high.astype(jnp.float32)).astype(jnp.bfloat16)


def dot(left, right):
    return jnp.dot(left, right, preferred_element_type=jnp.float32)


def dot3(left, right):
    return dot(left[0], right[0]) + (dot(left[0], right[1]) + dot(left[1], right[0]))


def panel_of(view, panel):
    rows = view.shape[0] // 8
    halves = [view[pl.ds(4 * half + panel, rows, stride=8), :] for half in range(2)]
    return jnp.concatenate(halves, 1)


def eighths(array):
    rows = array.size // (K * NB)
    return array.reshape(rows, K, 2, LANES).transpose(0, 2, 1, 3).reshape(rows * 8, LANES)


def take_body(panels, view, extra, out):
    rows = view.shape[0] // 8
    for at, panel in enumerate(panels):
        out[:rows, at * NB : (at + 1) * NB] = panel_of(view, panel)
    if extra is not None:
        out[rows:, :] = extra[...]


def take(panels, view, extra):
    rows = view.shape[0] // 8
    width = len(panels) * NB
    if extra is None:
        return call(
            lambda v, o: take_body(panels, v, None, o), struct(rows, width), (0, 2 * view.size)
        )(view)
    return call(
        lambda v, e, o: take_body(panels, v, e, o),
        struct(rows + extra.shape[0], width),
        (0, 2 * view.size),
    )(view, extra)


def turn_body(order, block, high, low):
    rows = block.shape[0] * block.shape[2] // 8
    flat = block.reshape(rows * 8, LANES)
    for part in range(8):
        value = flat[pl.ds(part, rows, stride=8), :].T
        top, rest = split(value)
        high[part * LANES : (part + 1) * LANES, :] = top
        low[part * LANES : (part + 1) * LANES, :] = rest


def turn(trail, order):
    cycles, slots, rows, _ = trail.shape
    unit = cycles * rows // 8
    spec = pl.BlockSpec((8 * LANES, unit), lambda i, order: (0, i))
    shape = struct(8 * LANES, slots * unit, dtype=jnp.bfloat16)
    return call(
        turn_body,
        (shape, shape),
        (0, 2 * trail.size * 4),
        grid_spec=pltpu.PrefetchScalarGridSpec(
            num_scalar_prefetch=1,
            grid=(slots,),
            in_specs=[
                pl.BlockSpec((cycles, 1, rows, LANES), lambda i, order: (0, order[i], 0, 0))
            ],
            out_specs=[spec, spec],
        ),
    )(order, trail)


def product_body(order, high, low, own, others, own_x, others_x, *rest):
    outs, (c_high, c_low, total) = rest[:4], rest[4:]
    unit = high.shape[1] // 8

    @pl.when(pl.program_id(0) == 0)
    def _():
        for half, (first, later) in enumerate(((own, others), (own_x, others_x))):
            for slot in range(NZ):
                value = first[:unit, :] if slot == 0 else later[slot - 1, :unit, :]
                at = pl.ds((half * NZ + slot) * unit, unit)
                c_high[at, :], c_low[at, :] = split(value)

    total[...] = dot3((high[...], low[...]), (c_high[...], c_low[...]))
    span = total.shape[0] // NZ
    for d in range(4):
        outs[d][0] = total[pl.ds(pl.multiple_of(order[d] * span, span), span), :]


def product(turned, order, own, others, own_x, others_x):
    high, low = turned
    rows, depth = high.shape
    width = own.shape[1]
    steps = rows // NB
    spec = pl.BlockSpec((NB, depth), lambda i, order: (i, 0))

    def whole(array):
        return pl.BlockSpec(array.shape, lambda i, order: (0,) * array.ndim)

    arrays = (own, others, own_x, others_x)
    span = NB // NZ
    return call(
        product_body,
        [struct(steps, span, width)] * 4,
        (6 * rows * depth * width, rows * depth * 4 + depth * width * 4),
        grid_spec=pltpu.PrefetchScalarGridSpec(
            num_scalar_prefetch=1,
            grid=(steps,),
            in_specs=[spec, spec] + [whole(a) for a in arrays],
            out_specs=[pl.BlockSpec((1, span, width), lambda i, order: (i, 0, 0))] * 4,
            scratch_shapes=[
                pltpu.VMEM((depth, width), jnp.bfloat16),
                pltpu.VMEM((depth, width), jnp.bfloat16),
                pltpu.VMEM((NB, width), jnp.float32),
            ],
        ),
    )(order, high, low, *arrays)


def smem():
    return pl.BlockSpec(memory_space=pltpu.SMEM)


def vmem():
    return pl.BlockSpec(memory_space=pltpu.VMEM)


def lay_top_body(where, lines, planes, planes_x, own_x, others_x, high, low, scratch):
    prow, layer, core = where[0], where[1], where[2]
    blocks = scratch.shape[0]
    rows = lines.shape[1]
    skip = own_x.shape[0] - rows
    share = rows // (blocks // 2)
    sub = 4 * share
    for far in range(2):
        for slot in range(NZ):
            for d in range(4):
                column = ((layer + slot) % NZ) * 2 + (core ^ far)
                at = pl.multiple_of(column * sub + (prow ^ d) * share, share)
                for block in range(blocks):
                    start = (block % (blocks // 2)) * share
                    lanes = slice(block // (blocks // 2) * NB, (block // (blocks // 2) + 1) * NB)
                    if d > 0:
                        source = planes_x if far else planes
                        value = source[d - 1, slot, start : start + share, lanes]
                    elif not far:
                        value = lines[slot, start : start + share, lanes]
                    elif slot == 0:
                        value = own_x[skip + start : skip + start + share, lanes]
                    else:
                        value = others_x[slot - 1, skip + start : skip + start + share, lanes]
                    scratch[block, pl.ds(at, share), :] = value
    for block in range(blocks):
        high[block], low[block] = split(scratch[block])


def lay_top(where, blocks, lines, planes, planes_x, own_x, others_x):
    shape = struct(blocks, NB, NB, dtype=jnp.bfloat16)
    return call(
        lay_top_body,
        (shape, shape),
        (0, 3 * blocks * NB * NB * 4),
        in_specs=[smem()] + [vmem()] * 5,
        out_specs=[vmem()] * 2,
        scratch_shapes=[pltpu.VMEM((blocks, NB, NB), jnp.float32)],
    )(where, lines, planes, planes_x, own_x, others_x)


def panel_body(panels, done, *refs):
    where, same, cross, adjoint, factor, top_high, top_low, adjoint_top = refs[:8]
    refs = refs[8:]
    lower_in, refs = refs[: len(done)], refs[len(done) :]
    blocks_in, refs = refs[: bool(done)], refs[bool(done) :]
    last = 0 in panels
    if last:
        grad, keep, send, image, scratch = refs
        lower_out = blocks_out = None
    else:
        lower_out, refs = refs[: len(panels)], refs[len(panels) :]
        blocks_out, keep, send, image, scratch = refs
    prow, pcol, core = where[0], where[1], where[2]
    steps = same.shape[0]
    sub = same.shape[1]
    for k in range(steps):
        image[pl.ds(pl.multiple_of((2 * k + core) * sub, sub), sub), :] = same[k]
        image[pl.ds(pl.multiple_of((2 * k + 1 - core) * sub, sub), sub), :] = cross[k]

    def block(row, column):
        slot = block_slot(row, column)
        return top_high[slot], top_low[slot]

    def block_row(row, columns):
        parts = [block(row, column) for column in range(columns)]
        return tuple(jnp.concatenate([part[i] for part in parts], 1) for i in range(2))

    def inverse(panel):
        slot = block_slot(K, 0) + panel
        return top_high[slot], top_low[slot]

    lower, parts = {}, {}
    for at, panel in enumerate(done):
        lower[panel] = lower_in[at][...]
        parts[panel] = split(lower[panel])
    columns = [split(panel_of(factor, panel)) for panel in range(max(panels) + 1)]
    terms = {}
    for at, panel in enumerate(panels):
        residual = panel_of(adjoint, panel) - 2.0 * image[:, at * NB : (at + 1) * NB]
        for later in range(panel + 1, K):
            residual = residual - dot3(parts[later], block(later, panel))
        value = dot3(split(residual), inverse(panel))
        lower[panel] = value
        parts[panel] = split(value)
        turned = split(value.T)
        for earlier in range(panel + 1):
            terms[panel, earlier] = -dot3(turned, columns[earlier])
    if last:
        for panel in range(K):
            for half in range(2):
                grad[pl.ds(4 * half + panel, grad.shape[0] // 8, stride=8), :] = lower[panel][
                    :, half * LANES : (half + 1) * LANES
                ]
    else:
        for at, panel in enumerate(panels):
            lower_out[at][...] = lower[panel]

    share = adjoint_top.shape[1]
    mine = jnp.where(prow == 0, 1.0, 0.0)
    upper, diag = {}, {}
    if done:
        slots = sorted(block_slot(r, c) for r in done for c in range(r + 1))
        for r in done:
            for c in range(r):
                upper[c, r] = blocks_in[0][slots.index(block_slot(r, c))]
    rows = {}
    for row in panels:
        flipped = {b: split(upper[row, b].T) for b in range(row + 1, K)}
        total = []
        for column in range(row + 1):
            scratch[...] = terms[row, column]
            at = pl.ds(pl.multiple_of(pcol * share, share), share)
            scratch[at, :] = scratch[at, :] + mine * adjoint_top[block_slot(row, column)]
            total.append(scratch[...])
        for b in range(row + 1, K):
            for column in range(row + 1):
                total[column] = total[column] - dot3(flipped[b], block(b, column))
        ids = [lax.broadcasted_iota(jnp.int32, (NB, NB), axis) for axis in range(2)]
        lower_adj = jnp.where(ids[0] >= ids[1], total[row], 0.0)
        d_high, d_low = block(row, row)
        factor_block = d_high.astype(jnp.float32) + d_low.astype(jnp.float32)
        factor_block = jnp.where(ids[0] >= ids[1], factor_block, 0.0).T
        inner = dot3(split(factor_block), split(lower_adj))
        inner = jnp.where(ids[0] > ids[1], inner, jnp.where(ids[0] == ids[1], 0.5 * inner, 0.0))
        i_high, i_low = inverse(row)
        turned = (i_high.astype(jnp.float32) + i_low.astype(jnp.float32)).T
        spread = dot3(split(turned), split(dot3(split(inner), inverse(row))))
        diag[row] = 0.5 * (spread + spread.T)
        doubled = split(2.0 * diag[row])
        for column in range(row):
            total[column] = total[column] - dot3(doubled, block(row, column))
        for column in reversed(range(row)):
            for middle in range(column + 1, row):
                total[column] = total[column] - dot3(split(upper[middle, row]), block(middle, column))
            upper[column, row] = dot3(split(total[column]), inverse(column))
        for column in range(row):
            rows[row, column] = upper[column, row]
        rows[row, row] = diag[row]
    for at, key in enumerate(sorted(rows)):
        scratch[...] = rows[key]
        if blocks_out is not None:
            blocks_out[at] = rows[key]
        for z in range(NZ):
            for target, which in ((keep, core), (send, 1 - core)):
                start = pl.multiple_of(z * 2 * share + which * share, share)
                target[at, z] = scratch[pl.ds(start, share), :]


def panel_group(panels, done, where, same, cross, views, top, adjoint_top, lower, blocks):
    local_rows = views[0].shape[0] // 8
    share = adjoint_top.shape[1]
    count = sum(panel + 1 for panel in panels)
    scattered = [struct(count, NZ, share, NB)] * 2
    if 0 in panels:
        out = [struct(*views[0].shape)] + scattered
    else:
        out = [struct(local_rows, NB)] * len(panels) + [struct(count, NB, NB)] + scattered
    arrays = (where, same, cross, *views, *top, adjoint_top, *lower, *blocks)
    work = 40 * 6 * NB**3
    return call(
        lambda *refs: panel_body(panels, done, *refs),
        out,
        (work, 10 * 1024 * 1024),
        in_specs=[smem()] + [vmem()] * (len(arrays) - 1),
        out_specs=[vmem()] * len(out),
        scratch_shapes=[
            pltpu.VMEM((local_rows, len(panels) * NB), jnp.float32),
            pltpu.VMEM((NB, NB), jnp.float32),
        ],
    )(*arrays)


def line_gather(piece):
    up, down = [piece], [piece]
    for _ in range(NZ - 1):
        up.append(move(up[-1], UP))
        down.append(move(down[-1], DOWN))
    return jnp.stack([down[t] + up[NZ - t] for t in range(1, NZ)])


def per_device(adjoint_trail, factor_low, adjoint_low, factor_top, adjoint_top, diag_inverse):
    cycles, sub_rows = factor_low.shape[0], factor_low.shape[3]
    col_cycles = adjoint_trail.shape[3]
    prow, pcol = lax.axis_index("prow"), lax.axis_index("pcol")
    layer, core = pcol // 2, pcol % 2
    holds = jnp.array(HOLDS, jnp.int32)
    shares = factor_top.shape[1]
    count = factor_top.shape[0]
    where = jnp.stack([prow, pcol, core]).astype(jnp.int32)
    order = jnp.stack([((layer + t) % NZ) * 2 + (core ^ f) for f in range(2) for t in range(NZ)])
    quarter = jnp.stack([holds[prow ^ d, layer] for d in range(4)])

    views = (eighths(adjoint_low), eighths(factor_low))
    part = shares // 4
    top_all = jnp.concatenate([factor_top, diag_inverse])
    total_blocks = top_all.shape[0]
    extra = pick(top_all.reshape(total_blocks, 4, part, NB), prow, 1)
    extra = extra.reshape(2, total_blocks // 2 * part, NB)
    extra = jnp.concatenate([extra[0], extra[1]], 1)

    pieces = [
        take(panels, views[1], extra if at == 0 else None) for at, panels in enumerate(GROUPS)
    ]
    gathered = [line_gather(piece) for piece in pieces]
    trail = adjoint_trail.reshape(cycles, 2 * NZ, sub_rows * 8, LANES)
    turned = turn(trail, order.astype(jnp.int32))

    rows = cycles * sub_rows
    lower, lower_of, blocks, scattered, low_out = [], [], [], [], None
    top = None
    for at, panels in enumerate(GROUPS):
        own, others = pieces[at], gathered[at]
        own_x, others_x = move(own, CORE), move(others, CORE)
        if at == 0:
            lines = jnp.concatenate([own[None, rows:], others[:, rows:]])
            planes = jnp.stack([move(lines, PLANE[d]) for d in (1, 2, 3)])
            planes_x = move(planes, CORE)
            spot = jnp.stack([prow, layer, core]).astype(jnp.int32)
            top = lay_top(spot, total_blocks, lines, planes, planes_x, own_x, others_x)
        outs = product(turned, quarter, own, others, own_x, others_x)
        total = outs[0] + sum(move(outs[d], PLANE[d]) for d in (1, 2, 3))
        total = total.reshape(col_cycles, 2, sub_rows, -1)
        same = move(pick(total, layer // 2, 1), HOME[0])
        cross = move(pick(total, 1 - layer // 2, 1), HOME[1])
        results = panel_group(
            panels, tuple(lower_of), where, same, cross, views, top, adjoint_top, lower, blocks
        )
        if 0 in panels:
            low_out = results[0]
        else:
            lower.extend(results[: len(panels)])
            lower_of.extend(panels)
            blocks = [results[len(panels)]]
        keep, send = results[-2:]
        kept = keep + move(send, CORE)
        line = pick(kept, layer, 1)
        for d in (1, 2, 3):
            line = line + move(pick(kept, layer ^ d, 1), LINE[d])
        scattered.append(line + sum(move(line, PLANE[d]) for d in (1, 2, 3)))
    grad_top = jnp.concatenate(scattered[::-1])
    grad_low = low_out.reshape(rows, 2, K, LANES).transpose(0, 2, 1, 3).reshape(factor_low.shape)
    return (grad_low, grad_top)


def covers(mesh):
    return mesh.shape["prow"] == 4 and mesh.shape["pcol"] == 8


def solution(mesh):
    in_specs = (
        P(None, "prow", None, None, "pcol", None),
        P(None, "prow", "pcol", None, None, None),
        P(None, "prow", "pcol", None, None, None),
        P(None, "pcol", None),
        P(None, "pcol", None),
        P(None, "pcol", None),
    )
    out_specs = (P(None, "prow", "pcol", None, None, None), P(None, "pcol", None))
    return jax.shard_map(
        per_device if covers(mesh) else per_device_any, mesh=mesh, in_specs=in_specs, out_specs=out_specs, check_vma=False
    )
```

```python
import jax
import jax.numpy as jnp
from jax import lax
from jax.experimental import pallas as pl
from jax.experimental.pallas import tpu as pltpu
from jax.sharding import PartitionSpec as P

NB = 256
K = 4


HIGHEST = lax.Precision.HIGHEST


def from_root(array, axis, root):
    mine = lax.axis_index(axis) == root
    return lax.psum(jnp.where(mine, array, jnp.zeros_like(array)), axis)


def matmul(left, right):
    return jnp.dot(left, right, precision=HIGHEST, preferred_element_type=jnp.float32)


def inner_product(left, right):
    return lax.dot_general(
        left, right, (((0,), (0,)), ((), ())), precision=HIGHEST, preferred_element_type=jnp.float32
    )


def block_slot(row_block, col_block):
    return row_block * (row_block + 1) // 2 + col_block


def half_lower(square):
    size = square.shape[0]
    row_ids = lax.broadcasted_iota(jnp.int32, (size, size), 0)
    col_ids = lax.broadcasted_iota(jnp.int32, (size, size), 1)
    return jnp.where(row_ids > col_ids, square, jnp.where(row_ids == col_ids, 0.5 * square, 0.0))


def diagonal_adjoint(diagonal, inverse, lower_adj):
    inner = half_lower(inner_product(jnp.tril(diagonal), lower_adj))
    spread = inner_product(inverse, matmul(inner, inverse))
    return 0.5 * (spread + spread.T)


def rows_one(piece):
    return lax.all_gather(piece, "pcol", axis=1, tiled=True)


def owner_one(piece, root):
    return from_root(piece, "prow", root)


def reduce_one(term, count):
    return lax.psum_scatter(
        term(jnp.int32(0), lax.axis_size("pcol") * count), "pcol", scatter_dimension=0, tiled=True
    )


def trailing_product(trail, panels, gather_rows, send_owner, reduce_rows):
    prow_count = lax.axis_size("prow")
    pcol_count = lax.axis_size("pcol")
    cycles, sub_rows, width = panels.shape
    block = sub_rows * pcol_count
    gathered = gather_rows(panels[:, None]).reshape(cycles, block, width)
    column = lax.axis_index("pcol")
    col_cycles = trail.shape[3]
    owned = []
    for cycle in range(col_cycles):
        global_block = cycle * pcol_count + column
        share = lax.dynamic_index_in_dim(gathered, global_block // prow_count, 0, keepdims=False)
        owned.append(send_owner(share, global_block % prow_count))
    stacked = jnp.stack(owned)
    view = trail.reshape(cycles, pcol_count, sub_rows, col_cycles, block)
    unit = cycles * sub_rows

    def term(start, count):
        product = jnp.einsum(
            "iaekb,kbn->aien", view, stacked, precision=HIGHEST, preferred_element_type=jnp.float32
        )
        return product.reshape(count, width)

    return reduce_rows(term, unit).reshape(cycles, sub_rows, width)


def per_device_any(adjoint_trail, factor_low, adjoint_low, factor_top, adjoint_top, diag_inverse):
    cycles = factor_low.shape[0]
    sub_rows = factor_low.shape[3]
    local_rows = cycles * sub_rows
    low_factor = factor_low.reshape(cycles, sub_rows, K * NB)
    low_adjoint = adjoint_low.reshape(local_rows, K, NB)
    columns = low_factor.reshape(local_rows, K, NB)
    top_factor, top_adjoint, inverses = (
        lax.all_gather(factor_top, "pcol", axis=1, tiled=True),
        lax.all_gather(adjoint_top, "pcol", axis=1, tiled=True),
        lax.all_gather(diag_inverse, "pcol", axis=1, tiled=True),
    )
    lower_grads = [None] * K
    diag_grads = [None] * K
    upper_grads = {}
    grams = {}

    def lower_step(panel):
        single = low_factor[:, :, panel * NB : (panel + 1) * NB]
        image = trailing_product(adjoint_trail, single, rows_one, owner_one, reduce_one).reshape(
            local_rows, NB
        )
        residual = low_adjoint[:, panel] - 2.0 * image
        for later in range(panel + 1, K):
            residual = residual - matmul(lower_grads[later], top_factor[block_slot(later, panel)])
        lower_grads[panel] = matmul(residual, inverses[panel])

    def top_step(panel):
        for row_block in range(panel + 1, K):
            top_residual = top_adjoint[block_slot(row_block, panel)] - grams[row_block, panel]
            top_residual = top_residual - 2.0 * matmul(
                diag_grads[row_block], top_factor[block_slot(row_block, panel)]
            )
            for middle in range(panel + 1, row_block):
                top_residual = top_residual - matmul(
                    upper_grads[middle, row_block], top_factor[block_slot(middle, panel)]
                )
            for beyond in range(row_block + 1, K):
                top_residual = top_residual - inner_product(
                    upper_grads[row_block, beyond], top_factor[block_slot(beyond, panel)]
                )
            upper_grads[panel, row_block] = matmul(top_residual, inverses[panel])
        lower_adj = top_adjoint[block_slot(panel, panel)] - grams[panel, panel]
        for row_block in range(panel + 1, K):
            lower_adj = lower_adj - inner_product(
                upper_grads[panel, row_block], top_factor[block_slot(row_block, panel)]
            )
        diag_grads[panel] = diagonal_adjoint(
            top_factor[block_slot(panel, panel)], inverses[panel], jnp.tril(lower_adj)
        )

    for panel in reversed(range(K)):
        lower_step(panel)
        local_gram = jnp.stack(
            [inner_product(lower_grads[panel], columns[:, earlier]) for earlier in range(panel + 1)]
        )
        summed = lax.psum(local_gram, ("prow", "pcol"))
        for earlier in range(panel + 1):
            grams[panel, earlier] = summed[earlier]
        top_step(panel)
    grad_low = jnp.stack(lower_grads, 1).reshape(factor_low.shape)
    blocks = []
    for row_block in range(K):
        for col_block in range(row_block + 1):
            if row_block == col_block:
                blocks.append(diag_grads[col_block])
            else:
                blocks.append(upper_grads[col_block, row_block])
    full_top = jnp.stack(blocks)
    share_rows = factor_top.shape[1]
    grad_top = lax.dynamic_slice_in_dim(
        full_top, lax.axis_index("pcol") * share_rows, share_rows, 1
    )
    return (grad_low, grad_top)


AXES = ("prow", "pcol")
NZ = 4
LANES = 128
VMEM = 48 * 1024 * 1024
GROUPS = ((3, 2), (1, 0))
HOLDS = ((0, 2, 1, 3), (1, 3, 0, 2), (2, 0, 3, 1), (3, 1, 2, 0))


def route(place):
    pairs = []
    for prow in range(4):
        for pcol in range(8):
            goal = place(prow, pcol // 2, pcol % 2)
            if goal is not None:
                pairs.append((prow * 8 + pcol, goal[0] * 8 + goal[1] * 2 + goal[2]))
    return pairs


CORE = route(lambda p, z, c: (p, z, 1 - c))
UP = route(lambda p, z, c: (p, z + 1, c) if z + 1 < NZ else None)
DOWN = route(lambda p, z, c: (p, z - 1, c) if z > 0 else None)
PLANE = {d: route(lambda p, z, c, d=d: (p ^ d, z, c)) for d in (1, 2, 3)}
LINE = {d: route(lambda p, z, c, d=d: (p, z ^ d, c)) for d in (1, 2, 3)}
HOME = {
    s: route(lambda p, z, c, s=s: ((z % 2) * 2 + c, HOLDS[p][z], (z // 2) ^ s)) for s in (0, 1)
}

BACK = {s: [(goal, source) for source, goal in HOME[s]] for s in (0, 1)}
SUM_UP = {t: route(lambda p, z, c, t=t: (p, z + 1, c) if z < min(t, 3) else None) for t in (1, 2, 3)}
SUM_DOWN = {
    t: route(lambda p, z, c, t=t: (p, z - 1, c) if z >= max(NZ - t, 1) else None) for t in (1, 2, 3)
}


def move(array, pairs):
    return lax.ppermute(array, AXES, pairs)


def pick(array, index, axis):
    return lax.dynamic_index_in_dim(array, index, axis, keepdims=False)


def call(body, out, cost, **more):
    flops, bytes_accessed = cost
    return pl.pallas_call(
        body,
        out_shape=out,
        compiler_params=pltpu.CompilerParams(vmem_limit_bytes=VMEM),
        cost_estimate=pl.CostEstimate(
            flops=flops, bytes_accessed=bytes_accessed, transcendentals=0
        ),
        **more,
    )


def struct(*shape, dtype=jnp.float32):
    return jax.ShapeDtypeStruct(shape, dtype)


def split(value):
    high = value.astype(jnp.bfloat16)
    return high, (value - high.astype(jnp.float32)).astype(jnp.bfloat16)


def dot(left, right):
    return jnp.dot(left, right, preferred_element_type=jnp.float32)


def dot3(left, right):
    return dot(left[0], right[0]) + (dot(left[0], right[1]) + dot(left[1], right[0]))


def panel_of(view, panel):
    rows = view.shape[0] // 8
    halves = [view[pl.ds(4 * half + panel, rows, stride=8), :] for half in range(2)]
    return jnp.concatenate(halves, 1)


def eighths(array):
    rows = array.size // (K * NB)
    return array.reshape(rows, K, 2, LANES).transpose(0, 2, 1, 3).reshape(rows * 8, LANES)


def take_body(panels, view, extra, out):
    rows = view.shape[0] // 8
    for at, panel in enumerate(panels):
        out[:rows, at * NB : (at + 1) * NB] = panel_of(view, panel)
    if extra is not None:
        out[rows:, :] = extra[...]


def take(panels, view, extra):
    rows = view.shape[0] // 8
    width = len(panels) * NB
    if extra is None:
        return call(
            lambda v, o: take_body(panels, v, None, o), struct(rows, width), (0, 2 * view.size)
        )(view)
    return call(
        lambda v, e, o: take_body(panels, v, e, o),
        struct(rows + extra.shape[0], width),
        (0, 2 * view.size),
    )(view, extra)


def take_parts_body(panels, core, view, same, cross, scratch):
    steps, sub = same.shape[0], same.shape[1]
    for at, panel in enumerate(panels):
        scratch[:, at * NB : (at + 1) * NB] = panel_of(view, panel)
    for k in range(steps):
        for out, odd in ((same, core[0]), (cross, 1 - core[0])):
            out[k] = scratch[pl.ds(pl.multiple_of((2 * k + odd) * sub, sub), sub), :]


def take_parts(panels, core, view, sub):
    rows, width = view.shape[0] // 8, len(panels) * NB
    shape = struct(rows // sub // 2, sub, width)
    return call(
        lambda *refs: take_parts_body(panels, *refs),
        [shape, shape],
        (0, 2 * view.size),
        in_specs=[smem(), vmem()],
        out_specs=[vmem(), vmem()],
        scratch_shapes=[pltpu.VMEM((rows, width), jnp.float32)],
    )(core, view)


def halve_body(order, block, high, low):
    rows = block.shape[0] * block.shape[2] // 8
    flat = block.reshape(rows * 8, LANES)
    for part in range(8):
        lanes = slice(part * LANES, (part + 1) * LANES)
        high[0, :, lanes], low[0, :, lanes] = split(flat[pl.ds(part, rows, stride=8), :])


def halve(trail, order):
    cycles, slots, rows, _ = trail.shape
    unit = cycles * rows // 8
    spec = pl.BlockSpec((1, unit, 8 * LANES), lambda i, order: (i, 0, 0))
    shape = struct(slots, unit, 8 * LANES, dtype=jnp.bfloat16)
    return call(
        halve_body,
        (shape, shape),
        (0, 2 * trail.size * 4),
        grid_spec=pltpu.PrefetchScalarGridSpec(
            num_scalar_prefetch=1,
            grid=(slots,),
            in_specs=[
                pl.BlockSpec((cycles, 1, rows, LANES), lambda i, order: (0, order[i], 0, 0))
            ],
            out_specs=[spec, spec],
        ),
    )(order, trail)


def column_body(where, high, low, *refs):
    quarters, out, c_high, c_low = refs[:8], refs[8], refs[9], refs[10]

    @pl.when(pl.program_id(0) == 0)
    def _():
        for d in range(4):
            for side in range(2):
                source = quarters[2 * d + side]
                sub = source.shape[1]
                for k in range(source.shape[0]):
                    at = k * NB + (where[d] * 2 + (where[4] ^ side)) * sub
                    at = pl.ds(pl.multiple_of(at, sub), sub)
                    c_high[at, :], c_low[at, :] = split(source[k])

    out[0] = dot3((high[0], low[0]), (c_high[...], c_low[...]))


def column_product(halves, first, count, where, quarters):
    unit, depth = halves[0].shape[1:]
    width = quarters[0].shape[2]
    spec = pl.BlockSpec((1, unit, depth), lambda i, where: (first + i, 0, 0))
    whole = [pl.BlockSpec(q.shape, lambda i, where: (0, 0, 0)) for q in quarters]
    return call(
        column_body,
        struct(count, unit, width),
        (6 * count * unit * depth * width, count * unit * depth * 4 + depth * width * 4),
        grid_spec=pltpu.PrefetchScalarGridSpec(
            num_scalar_prefetch=1,
            grid=(count,),
            in_specs=[spec, spec] + whole,
            out_specs=pl.BlockSpec((1, unit, width), lambda i, where: (i, 0, 0)),
            scratch_shapes=[pltpu.VMEM((depth, width), jnp.bfloat16)] * 2,
        ),
    )(where, *halves, *quarters)


def turn_body(order, block, high, low):
    rows = block.shape[0] * block.shape[2] // 8
    flat = block.reshape(rows * 8, LANES)
    for part in range(8):
        value = flat[pl.ds(part, rows, stride=8), :].T
        top, rest = split(value)
        high[part * LANES : (part + 1) * LANES, :] = top
        low[part * LANES : (part + 1) * LANES, :] = rest


def turn(trail, order):
    cycles, slots, rows, _ = trail.shape
    unit = cycles * rows // 8
    spec = pl.BlockSpec((8 * LANES, unit), lambda i, order: (0, i))
    shape = struct(8 * LANES, slots * unit, dtype=jnp.bfloat16)
    return call(
        turn_body,
        (shape, shape),
        (0, 2 * trail.size * 4),
        grid_spec=pltpu.PrefetchScalarGridSpec(
            num_scalar_prefetch=1,
            grid=(slots,),
            in_specs=[
                pl.BlockSpec((cycles, 1, rows, LANES), lambda i, order: (0, order[i], 0, 0))
            ],
            out_specs=[spec, spec],
        ),
    )(order, trail)


def product_body(order, high, low, own, others, own_x, others_x, *rest):
    outs, (c_high, c_low, total) = rest[:4], rest[4:]
    unit = high.shape[1] // 8

    @pl.when(pl.program_id(0) == 0)
    def _():
        for half, (first, later) in enumerate(((own, others), (own_x, others_x))):
            for slot in range(NZ):
                value = first[:unit, :] if slot == 0 else later[slot - 1, :unit, :]
                at = pl.ds((half * NZ + slot) * unit, unit)
                c_high[at, :], c_low[at, :] = split(value)

    total[...] = dot3((high[...], low[...]), (c_high[...], c_low[...]))
    span = total.shape[0] // NZ
    for d in range(4):
        outs[d][0] = total[pl.ds(pl.multiple_of(order[d] * span, span), span), :]


def product(turned, order, own, others, own_x, others_x):
    high, low = turned
    rows, depth = high.shape
    width = own.shape[1]
    steps = rows // NB
    spec = pl.BlockSpec((NB, depth), lambda i, order: (i, 0))

    def whole(array):
        return pl.BlockSpec(array.shape, lambda i, order: (0,) * array.ndim)

    arrays = (own, others, own_x, others_x)
    span = NB // NZ
    return call(
        product_body,
        [struct(steps, span, width)] * 4,
        (6 * rows * depth * width, rows * depth * 4 + depth * width * 4),
        grid_spec=pltpu.PrefetchScalarGridSpec(
            num_scalar_prefetch=1,
            grid=(steps,),
            in_specs=[spec, spec] + [whole(a) for a in arrays],
            out_specs=[pl.BlockSpec((1, span, width), lambda i, order: (i, 0, 0))] * 4,
            scratch_shapes=[
                pltpu.VMEM((depth, width), jnp.bfloat16),
                pltpu.VMEM((depth, width), jnp.bfloat16),
                pltpu.VMEM((NB, width), jnp.float32),
            ],
        ),
    )(order, high, low, *arrays)


def smem():
    return pl.BlockSpec(memory_space=pltpu.SMEM)


def vmem():
    return pl.BlockSpec(memory_space=pltpu.VMEM)


def lay_top_body(where, lines, planes, planes_x, own_x, others_x, high, low, scratch):
    prow, layer, core = where[0], where[1], where[2]
    blocks = scratch.shape[0]
    rows = lines.shape[1]
    skip = own_x.shape[0] - rows
    share = rows // (blocks // 2)
    sub = 4 * share
    for far in range(2):
        for slot in range(NZ):
            for d in range(4):
                column = ((layer + slot) % NZ) * 2 + (core ^ far)
                at = pl.multiple_of(column * sub + (prow ^ d) * share, share)
                for block in range(blocks):
                    start = (block % (blocks // 2)) * share
                    lanes = slice(block // (blocks // 2) * NB, (block // (blocks // 2) + 1) * NB)
                    if d > 0:
                        source = planes_x if far else planes
                        value = source[d - 1, slot, start : start + share, lanes]
                    elif not far:
                        value = lines[slot, start : start + share, lanes]
                    elif slot == 0:
                        value = own_x[skip + start : skip + start + share, lanes]
                    else:
                        value = others_x[slot - 1, skip + start : skip + start + share, lanes]
                    scratch[block, pl.ds(at, share), :] = value
    for block in range(blocks):
        high[block], low[block] = split(scratch[block])


def lay_top(where, blocks, lines, planes, planes_x, own_x, others_x):
    shape = struct(blocks, NB, NB, dtype=jnp.bfloat16)
    return call(
        lay_top_body,
        (shape, shape),
        (0, 3 * blocks * NB * NB * 4),
        in_specs=[smem()] + [vmem()] * 5,
        out_specs=[vmem()] * 2,
        scratch_shapes=[pltpu.VMEM((blocks, NB, NB), jnp.float32)],
    )(where, lines, planes, planes_x, own_x, others_x)


def panel_body(panels, done, parts_in, *refs):
    where, refs = refs[0], refs[1:]
    images, refs = refs[:parts_in], refs[parts_in:]
    adjoint, factor, top_high, top_low, adjoint_top = refs[:5]
    refs = refs[5:]
    lower_in, refs = refs[: len(done)], refs[len(done) :]
    blocks_in, refs = refs[: bool(done)], refs[bool(done) :]
    last = 0 in panels
    if last:
        grad, keep, send, image, scratch = refs
        lower_out = blocks_out = None
    else:
        lower_out, refs = refs[: len(panels)], refs[len(panels) :]
        blocks_out, keep, send, image, scratch = refs
    prow, pcol, core = where[0], where[1], where[2]
    if parts_in == 2:
        same, cross = images
        steps, sub = same.shape[0], same.shape[1]
        for k in range(steps):
            image[pl.ds(pl.multiple_of((2 * k + core) * sub, sub), sub), :] = same[k]
            image[pl.ds(pl.multiple_of((2 * k + 1 - core) * sub, sub), sub), :] = cross[k]
    else:
        image[...] = images[0][...]

    def block(row, column):
        slot = block_slot(row, column)
        return top_high[slot], top_low[slot]

    def block_row(row, columns):
        parts = [block(row, column) for column in range(columns)]
        return tuple(jnp.concatenate([part[i] for part in parts], 1) for i in range(2))

    def inverse(panel):
        slot = block_slot(K, 0) + panel
        return top_high[slot], top_low[slot]

    lower, parts = {}, {}
    for at, panel in enumerate(done):
        lower[panel] = lower_in[at][...]
        parts[panel] = split(lower[panel])
    columns = [split(panel_of(factor, panel)) for panel in range(max(panels) + 1)]
    terms = {}
    for at, panel in enumerate(panels):
        residual = panel_of(adjoint, panel) - 2.0 * image[:, at * NB : (at + 1) * NB]
        for later in range(panel + 1, K):
            residual = residual - dot3(parts[later], block(later, panel))
        value = dot3(split(residual), inverse(panel))
        lower[panel] = value
        parts[panel] = split(value)
        turned = split(value.T)
        for earlier in range(panel + 1):
            terms[panel, earlier] = -dot3(turned, columns[earlier])
    if last:
        for panel in range(K):
            for half in range(2):
                grad[pl.ds(4 * half + panel, grad.shape[0] // 8, stride=8), :] = lower[panel][
                    :, half * LANES : (half + 1) * LANES
                ]
    else:
        for at, panel in enumerate(panels):
            lower_out[at][...] = lower[panel]

    share = adjoint_top.shape[1]
    mine = jnp.where(prow == 0, 1.0, 0.0)
    upper, diag = {}, {}
    if done:
        slots = sorted(block_slot(r, c) for r in done for c in range(r + 1))
        for r in done:
            for c in range(r):
                upper[c, r] = blocks_in[0][slots.index(block_slot(r, c))]
    rows = {}
    for row in panels:
        flipped = {b: split(upper[row, b].T) for b in range(row + 1, K)}
        total = []
        for column in range(row + 1):
            scratch[...] = terms[row, column]
            at = pl.ds(pl.multiple_of(pcol * share, share), share)
            scratch[at, :] = scratch[at, :] + mine * adjoint_top[block_slot(row, column)]
            total.append(scratch[...])
        for b in range(row + 1, K):
            for column in range(row + 1):
                total[column] = total[column] - dot3(flipped[b], block(b, column))
        ids = [lax.broadcasted_iota(jnp.int32, (NB, NB), axis) for axis in range(2)]
        lower_adj = jnp.where(ids[0] >= ids[1], total[row], 0.0)
        d_high, d_low = block(row, row)
        factor_block = d_high.astype(jnp.float32) + d_low.astype(jnp.float32)
        factor_block = jnp.where(ids[0] >= ids[1], factor_block, 0.0).T
        inner = dot3(split(factor_block), split(lower_adj))
        inner = jnp.where(ids[0] > ids[1], inner, jnp.where(ids[0] == ids[1], 0.5 * inner, 0.0))
        i_high, i_low = inverse(row)
        turned = (i_high.astype(jnp.float32) + i_low.astype(jnp.float32)).T
        spread = dot3(split(turned), split(dot3(split(inner), inverse(row))))
        diag[row] = 0.5 * (spread + spread.T)
        doubled = split(2.0 * diag[row])
        for column in range(row):
            total[column] = total[column] - dot3(doubled, block(row, column))
        for column in reversed(range(row)):
            for middle in range(column + 1, row):
                total[column] = total[column] - dot3(split(upper[middle, row]), block(middle, column))
            upper[column, row] = dot3(split(total[column]), inverse(column))
        for column in range(row):
            rows[row, column] = upper[column, row]
        rows[row, row] = diag[row]
    for at, key in enumerate(sorted(rows)):
        scratch[...] = rows[key]
        if blocks_out is not None:
            blocks_out[at] = rows[key]
        for z in range(NZ):
            for target, which in ((keep, core), (send, 1 - core)):
                start = pl.multiple_of(z * 2 * share + which * share, share)
                target[at, z] = scratch[pl.ds(start, share), :]


def panel_group(panels, done, where, images, views, top, adjoint_top, lower, blocks):
    local_rows = views[0].shape[0] // 8
    share = adjoint_top.shape[1]
    count = sum(panel + 1 for panel in panels)
    scattered = [struct(count, NZ, share, NB)] * 2
    if 0 in panels:
        out = [struct(*views[0].shape)] + scattered
    else:
        out = [struct(local_rows, NB)] * len(panels) + [struct(count, NB, NB)] + scattered
    arrays = (where, *images, *views, *top, adjoint_top, *lower, *blocks)
    work = 40 * 6 * NB**3
    return call(
        lambda *refs: panel_body(panels, done, len(images), *refs),
        out,
        (work, 10 * 1024 * 1024),
        in_specs=[smem()] + [vmem()] * (len(arrays) - 1),
        out_specs=[vmem()] * len(out),
        scratch_shapes=[
            pltpu.VMEM((local_rows, len(panels) * NB), jnp.float32),
            pltpu.VMEM((NB, NB), jnp.float32),
        ],
    )(*arrays)


def line_gather(piece):
    up, down = [piece], [piece]
    for _ in range(NZ - 1):
        up.append(move(up[-1], UP))
        down.append(move(down[-1], DOWN))
    return jnp.stack([down[t] + up[NZ - t] for t in range(1, NZ)])


def per_device(adjoint_trail, factor_low, adjoint_low, factor_top, adjoint_top, diag_inverse):
    cycles, sub_rows = factor_low.shape[0], factor_low.shape[3]
    col_cycles = adjoint_trail.shape[3]
    prow, pcol = lax.axis_index("prow"), lax.axis_index("pcol")
    layer, core = pcol // 2, pcol % 2
    holds = jnp.array(HOLDS, jnp.int32)
    shares = factor_top.shape[1]
    count = factor_top.shape[0]
    where = jnp.stack([prow, pcol, core]).astype(jnp.int32)
    order = jnp.stack([((layer + t) % NZ) * 2 + (core ^ f) for f in range(2) for t in range(NZ)])
    quarter = jnp.stack([holds[prow ^ d, layer] for d in range(4)])

    views = (eighths(adjoint_low), eighths(factor_low))
    part = shares // 4
    top_all = jnp.concatenate([factor_top, diag_inverse])
    total_blocks = top_all.shape[0]
    extra = pick(top_all.reshape(total_blocks, 4, part, NB), prow, 1)
    extra = extra.reshape(2, total_blocks // 2 * part, NB)
    extra = jnp.concatenate([extra[0], extra[1]], 1)

    rows = cycles * sub_rows
    trail = adjoint_trail.reshape(cycles, 2 * NZ, sub_rows * 8, LANES)
    spot = jnp.stack([prow, layer, core]).astype(jnp.int32)
    quarters = jnp.concatenate([quarter, (layer // 2)[None]]).astype(jnp.int32)
    near = jnp.stack([((layer + t) % NZ) * 2 + (core ^ 1 ^ f) for f in range(2) for t in range(NZ)])

    own = take(GROUPS[0], views[1], extra)
    mine = take_parts(GROUPS[1], core[None].astype(jnp.int32), views[1], sub_rows)
    mine = [move(mine[s], BACK[s]) for s in (0, 1)]
    others = line_gather(own)
    spread = list(mine)
    for d in (1, 2, 3):
        spread += [move(mine[s], PLANE[d]) for s in (0, 1)]
    halves = halve(trail, near.astype(jnp.int32))
    turned = turn(trail, order.astype(jnp.int32))
    send = column_product(halves, 0, NZ, quarters, spread)
    keep = column_product(halves, NZ, NZ, quarters, spread)
    crossed = move(send, CORE)
    partial = [keep[t] + crossed[t] for t in range(NZ)]
    up = down = None
    for t in (1, 2, 3):
        up_term, down_term = partial[NZ - t], partial[t]
        if t > 1:
            up_term, down_term = up_term + up, down_term + down
        up, down = move(up_term, SUM_UP[t]), move(down_term, SUM_DOWN[t])
    second_image = partial[0] + up + down

    own_x, others_x = move(own, CORE), move(others, CORE)
    lines = jnp.concatenate([own[None, rows:], others[:, rows:]])
    planes = jnp.stack([move(lines, PLANE[d]) for d in (1, 2, 3)])
    planes_x = move(planes, CORE)
    top = lay_top(spot, total_blocks, lines, planes, planes_x, own_x, others_x)
    outs = product(turned, quarter, own, others, own_x, others_x)
    total = outs[0] + sum(move(outs[d], PLANE[d]) for d in (1, 2, 3))
    total = total.reshape(col_cycles, 2, sub_rows, -1)
    same = move(pick(total, layer // 2, 1), HOME[0])
    cross = move(pick(total, 1 - layer // 2, 1), HOME[1])

    def scatter(keep, send):
        kept = keep + move(send, CORE)
        line = pick(kept, layer, 1)
        for d in (1, 2, 3):
            line = line + move(pick(kept, layer ^ d, 1), LINE[d])
        return line + sum(move(line, PLANE[d]) for d in (1, 2, 3))

    *lower, blocks, keep, send = panel_group(
        GROUPS[0], (), where, (same, cross), views, top, adjoint_top, (), ()
    )
    low_rows = scatter(keep, send)
    low_out, keep, send = panel_group(
        GROUPS[1], GROUPS[0], where, (second_image,), views, top, adjoint_top, lower, (blocks,)
    )
    grad_top = jnp.concatenate([scatter(keep, send), low_rows])
    grad_low = low_out.reshape(rows, 2, K, LANES).transpose(0, 2, 1, 3).reshape(factor_low.shape)
    return (grad_low, grad_top)


def covers(mesh):
    return mesh.shape["prow"] == 4 and mesh.shape["pcol"] == 8


def solution(mesh):
    in_specs = (
        P(None, "prow", None, None, "pcol", None),
        P(None, "prow", "pcol", None, None, None),
        P(None, "prow", "pcol", None, None, None),
        P(None, "pcol", None),
        P(None, "pcol", None),
        P(None, "pcol", None),
    )
    out_specs = (P(None, "prow", "pcol", None, None, None), P(None, "pcol", None))
    return jax.shard_map(
        per_device if covers(mesh) else per_device_any, mesh=mesh, in_specs=in_specs, out_specs=out_specs, check_vma=False
    )
```

```python
import jax
import jax.numpy as jnp
from jax import lax
from jax.experimental import pallas as pl
from jax.experimental.pallas import tpu as pltpu
from jax.sharding import PartitionSpec as P

NB = 256
K = 4


HIGHEST = lax.Precision.HIGHEST


def from_root(array, axis, root):
    mine = lax.axis_index(axis) == root
    return lax.psum(jnp.where(mine, array, jnp.zeros_like(array)), axis)


def matmul(left, right):
    return jnp.dot(left, right, precision=HIGHEST, preferred_element_type=jnp.float32)


def inner_product(left, right):
    return lax.dot_general(
        left, right, (((0,), (0,)), ((), ())), precision=HIGHEST, preferred_element_type=jnp.float32
    )


def block_slot(row_block, col_block):
    return row_block * (row_block + 1) // 2 + col_block


def half_lower(square):
    size = square.shape[0]
    row_ids = lax.broadcasted_iota(jnp.int32, (size, size), 0)
    col_ids = lax.broadcasted_iota(jnp.int32, (size, size), 1)
    return jnp.where(row_ids > col_ids, square, jnp.where(row_ids == col_ids, 0.5 * square, 0.0))


def diagonal_adjoint(diagonal, inverse, lower_adj):
    inner = half_lower(inner_product(jnp.tril(diagonal), lower_adj))
    spread = inner_product(inverse, matmul(inner, inverse))
    return 0.5 * (spread + spread.T)


def rows_one(piece):
    return lax.all_gather(piece, "pcol", axis=1, tiled=True)


def owner_one(piece, root):
    return from_root(piece, "prow", root)


def reduce_one(term, count):
    return lax.psum_scatter(
        term(jnp.int32(0), lax.axis_size("pcol") * count), "pcol", scatter_dimension=0, tiled=True
    )


def trailing_product(trail, panels, gather_rows, send_owner, reduce_rows):
    prow_count = lax.axis_size("prow")
    pcol_count = lax.axis_size("pcol")
    cycles, sub_rows, width = panels.shape
    block = sub_rows * pcol_count
    gathered = gather_rows(panels[:, None]).reshape(cycles, block, width)
    column = lax.axis_index("pcol")
    col_cycles = trail.shape[3]
    owned = []
    for cycle in range(col_cycles):
        global_block = cycle * pcol_count + column
        share = lax.dynamic_index_in_dim(gathered, global_block // prow_count, 0, keepdims=False)
        owned.append(send_owner(share, global_block % prow_count))
    stacked = jnp.stack(owned)
    view = trail.reshape(cycles, pcol_count, sub_rows, col_cycles, block)
    unit = cycles * sub_rows

    def term(start, count):
        product = jnp.einsum(
            "iaekb,kbn->aien", view, stacked, precision=HIGHEST, preferred_element_type=jnp.float32
        )
        return product.reshape(count, width)

    return reduce_rows(term, unit).reshape(cycles, sub_rows, width)


def per_device_any(adjoint_trail, factor_low, adjoint_low, factor_top, adjoint_top, diag_inverse):
    cycles = factor_low.shape[0]
    sub_rows = factor_low.shape[3]
    local_rows = cycles * sub_rows
    low_factor = factor_low.reshape(cycles, sub_rows, K * NB)
    low_adjoint = adjoint_low.reshape(local_rows, K, NB)
    columns = low_factor.reshape(local_rows, K, NB)
    top_factor, top_adjoint, inverses = (
        lax.all_gather(factor_top, "pcol", axis=1, tiled=True),
        lax.all_gather(adjoint_top, "pcol", axis=1, tiled=True),
        lax.all_gather(diag_inverse, "pcol", axis=1, tiled=True),
    )
    lower_grads = [None] * K
    diag_grads = [None] * K
    upper_grads = {}
    grams = {}

    def lower_step(panel):
        single = low_factor[:, :, panel * NB : (panel + 1) * NB]
        image = trailing_product(adjoint_trail, single, rows_one, owner_one, reduce_one).reshape(
            local_rows, NB
        )
        residual = low_adjoint[:, panel] - 2.0 * image
        for later in range(panel + 1, K):
            residual = residual - matmul(lower_grads[later], top_factor[block_slot(later, panel)])
        lower_grads[panel] = matmul(residual, inverses[panel])

    def top_step(panel):
        for row_block in range(panel + 1, K):
            top_residual = top_adjoint[block_slot(row_block, panel)] - grams[row_block, panel]
            top_residual = top_residual - 2.0 * matmul(
                diag_grads[row_block], top_factor[block_slot(row_block, panel)]
            )
            for middle in range(panel + 1, row_block):
                top_residual = top_residual - matmul(
                    upper_grads[middle, row_block], top_factor[block_slot(middle, panel)]
                )
            for beyond in range(row_block + 1, K):
                top_residual = top_residual - inner_product(
                    upper_grads[row_block, beyond], top_factor[block_slot(beyond, panel)]
                )
            upper_grads[panel, row_block] = matmul(top_residual, inverses[panel])
        lower_adj = top_adjoint[block_slot(panel, panel)] - grams[panel, panel]
        for row_block in range(panel + 1, K):
            lower_adj = lower_adj - inner_product(
                upper_grads[panel, row_block], top_factor[block_slot(row_block, panel)]
            )
        diag_grads[panel] = diagonal_adjoint(
            top_factor[block_slot(panel, panel)], inverses[panel], jnp.tril(lower_adj)
        )

    for panel in reversed(range(K)):
        lower_step(panel)
        local_gram = jnp.stack(
            [inner_product(lower_grads[panel], columns[:, earlier]) for earlier in range(panel + 1)]
        )
        summed = lax.psum(local_gram, ("prow", "pcol"))
        for earlier in range(panel + 1):
            grams[panel, earlier] = summed[earlier]
        top_step(panel)
    grad_low = jnp.stack(lower_grads, 1).reshape(factor_low.shape)
    blocks = []
    for row_block in range(K):
        for col_block in range(row_block + 1):
            if row_block == col_block:
                blocks.append(diag_grads[col_block])
            else:
                blocks.append(upper_grads[col_block, row_block])
    full_top = jnp.stack(blocks)
    share_rows = factor_top.shape[1]
    grad_top = lax.dynamic_slice_in_dim(
        full_top, lax.axis_index("pcol") * share_rows, share_rows, 1
    )
    return (grad_low, grad_top)


AXES = ("prow", "pcol")
NZ = 4
LANES = 128
VMEM = 48 * 1024 * 1024
GROUPS = ((3, 2), (1, 0))
HOLDS = ((0, 2, 1, 3), (1, 3, 0, 2), (2, 0, 3, 1), (3, 1, 2, 0))


def route(place):
    pairs = []
    for prow in range(4):
        for pcol in range(8):
            goal = place(prow, pcol // 2, pcol % 2)
            if goal is not None:
                pairs.append((prow * 8 + pcol, goal[0] * 8 + goal[1] * 2 + goal[2]))
    return pairs


CORE = route(lambda p, z, c: (p, z, 1 - c))
PLANE = {d: route(lambda p, z, c, d=d: (p ^ d, z, c)) for d in (1, 2, 3)}
LINE = {d: route(lambda p, z, c, d=d: (p, z ^ d, c)) for d in (1, 2, 3)}
MIDDLE_IN = route(lambda p, z, c: (p, z ^ 1, c) if z in (0, 3) else None)
MIDDLE_OUT = {d: route(lambda p, z, c, d=d: (p, z ^ d, c) if z in (1, 2) else None) for d in (2, 3)}
HOME = {
    s: route(lambda p, z, c, s=s: ((z % 2) * 2 + c, HOLDS[p][z], (z // 2) ^ s)) for s in (0, 1)
}

BACK = {s: [(goal, source) for source, goal in HOME[s]] for s in (0, 1)}


def move(array, pairs):
    return lax.ppermute(array, AXES, pairs)


def pick(array, index, axis):
    return lax.dynamic_index_in_dim(array, index, axis, keepdims=False)


def call(body, out, cost, **more):
    flops, bytes_accessed = cost
    return pl.pallas_call(
        body,
        out_shape=out,
        compiler_params=pltpu.CompilerParams(vmem_limit_bytes=VMEM),
        cost_estimate=pl.CostEstimate(
            flops=flops, bytes_accessed=bytes_accessed, transcendentals=0
        ),
        **more,
    )


def struct(*shape, dtype=jnp.float32):
    return jax.ShapeDtypeStruct(shape, dtype)


def split(value):
    high = value.astype(jnp.bfloat16)
    return high, (value - high.astype(jnp.float32)).astype(jnp.bfloat16)


def dot(left, right):
    return jnp.dot(left, right, preferred_element_type=jnp.float32)


def dot3(left, right):
    return dot(left[0], right[0]) + (dot(left[0], right[1]) + dot(left[1], right[0]))


def panel_of(view, panel):
    rows = view.shape[0] // 8
    halves = [view[pl.ds(4 * half + panel, rows, stride=8), :] for half in range(2)]
    return jnp.concatenate(halves, 1)


def eighths(array):
    rows = array.size // (K * NB)
    return array.reshape(rows, K, 2, LANES).transpose(0, 2, 1, 3).reshape(rows * 8, LANES)


def take_body(panels, view, extra, out):
    rows = view.shape[0] // 8
    for at, panel in enumerate(panels):
        out[:rows, at * NB : (at + 1) * NB] = panel_of(view, panel)
    if extra is not None:
        out[rows:, :] = extra[...]


def take(panels, view, extra):
    rows = view.shape[0] // 8
    width = len(panels) * NB
    if extra is None:
        return call(
            lambda v, o: take_body(panels, v, None, o), struct(rows, width), (0, 2 * view.size)
        )(view)
    return call(
        lambda v, e, o: take_body(panels, v, e, o),
        struct(rows + extra.shape[0], width),
        (0, 2 * view.size),
    )(view, extra)


def take_parts_body(panels, core, view, same, cross, scratch):
    steps, sub = same.shape[0], same.shape[1]
    for at, panel in enumerate(panels):
        scratch[:, at * NB : (at + 1) * NB] = panel_of(view, panel)
    for k in range(steps):
        for out, odd in ((same, core[0]), (cross, 1 - core[0])):
            out[k] = scratch[pl.ds(pl.multiple_of((2 * k + odd) * sub, sub), sub), :]


def take_parts(panels, core, view, sub):
    rows, width = view.shape[0] // 8, len(panels) * NB
    shape = struct(rows // sub // 2, sub, width)
    return call(
        lambda *refs: take_parts_body(panels, *refs),
        [shape, shape],
        (0, 2 * view.size),
        in_specs=[smem(), vmem()],
        out_specs=[vmem(), vmem()],
        scratch_shapes=[pltpu.VMEM((rows, width), jnp.float32)],
    )(core, view)


def halve_body(block, high, low):
    rows = block.shape[0] * block.shape[2] // 8
    flat = block.reshape(rows * 8, LANES)
    for part in range(8):
        lanes = slice(part * LANES, (part + 1) * LANES)
        high[0, :, lanes], low[0, :, lanes] = split(flat[pl.ds(part, rows, stride=8), :])


def halve(trail):
    cycles, slots, rows, _ = trail.shape
    unit = cycles * rows // 8
    spec = pl.BlockSpec((1, unit, 8 * LANES), lambda i: (i, 0, 0))
    shape = struct(slots, unit, 8 * LANES, dtype=jnp.bfloat16)
    return call(
        halve_body,
        (shape, shape),
        (0, 2 * trail.size * 4),
        grid=(slots,),
        in_specs=[pl.BlockSpec((cycles, 1, rows, LANES), lambda i: (0, i, 0, 0))],
        out_specs=[spec, spec],
    )(trail)


def column_body(where, high, low, *refs):
    quarters, out, c_high, c_low = refs[:4], refs[4], refs[5], refs[6]

    @pl.when(pl.program_id(0) == 0)
    def _():
        for d in range(4):
            for side in range(2):
                source = quarters[d]
                sub = source.shape[2]
                for k in range(source.shape[1]):
                    at = k * NB + (where[d] * 2 + ((where[4] // 2) ^ side)) * sub
                    at = pl.ds(pl.multiple_of(at, sub), sub)
                    c_high[at, :], c_low[at, :] = split(source[side, k])

    out[0] = dot3((high[0], low[0]), (c_high[...], c_low[...]))


def column_product(halves, side, where, quarters):
    unit, depth = halves[0].shape[1:]
    width = quarters[0].shape[3]

    def slot(i, where):
        return ((where[4] ^ i) * 2 + (where[5] ^ side), 0, 0)

    whole = [pl.BlockSpec(q.shape, lambda i, where: (0, 0, 0, 0)) for q in quarters]
    return call(
        column_body,
        struct(NZ, unit, width),
        (6 * NZ * unit * depth * width, NZ * unit * depth * 4 + depth * width * 4),
        grid_spec=pltpu.PrefetchScalarGridSpec(
            num_scalar_prefetch=1,
            grid=(NZ,),
            in_specs=[pl.BlockSpec((1, unit, depth), slot)] * 2 + whole,
            out_specs=pl.BlockSpec((1, unit, width), lambda i, where: (i, 0, 0)),
            scratch_shapes=[pltpu.VMEM((depth, width), jnp.bfloat16)] * 2,
        ),
    )(where, *halves, *quarters)


def turn_body(block, high, low):
    rows = block.shape[0] * block.shape[2] // 8
    flat = block.reshape(rows * 8, LANES)
    for part in range(8):
        value = flat[pl.ds(part, rows, stride=8), :].T
        top, rest = split(value)
        high[part * LANES : (part + 1) * LANES, :] = top
        low[part * LANES : (part + 1) * LANES, :] = rest


def turn(trail):
    cycles, slots, rows, _ = trail.shape
    unit = cycles * rows // 8
    spec = pl.BlockSpec((8 * LANES, unit), lambda i: (0, i))
    shape = struct(8 * LANES, slots * unit, dtype=jnp.bfloat16)
    return call(
        turn_body,
        (shape, shape),
        (0, 2 * trail.size * 4),
        grid=(slots,),
        in_specs=[pl.BlockSpec((cycles, 1, rows, LANES), lambda i: (0, i, 0, 0))],
        out_specs=[spec, spec],
    )(trail)


def product_body(where, high, low, near, far, *rest):
    outs, (c_high, c_low, total) = rest[:4], rest[4:]
    unit = high.shape[1] // (2 * NZ)

    @pl.when(pl.program_id(0) == 0)
    def _():
        for side, source in enumerate((near, far)):
            for d in range(NZ):
                at = ((where[4] ^ d) * 2 + (where[5] ^ side)) * unit
                at = pl.ds(pl.multiple_of(at, unit), unit)
                c_high[at, :], c_low[at, :] = split(source[d, :unit, :])

    total[...] = dot3((high[...], low[...]), (c_high[...], c_low[...]))
    span = total.shape[0] // NZ
    for d in range(4):
        outs[d][0] = total[pl.ds(pl.multiple_of(where[d] * span, span), span), :]


def product(turned, where, near, far):
    high, low = turned
    rows, depth = high.shape
    width = near.shape[2]
    steps = rows // NB
    span = NB // NZ
    spec = pl.BlockSpec((NB, depth), lambda i, where: (i, 0))
    whole = pl.BlockSpec(near.shape, lambda i, where: (0, 0, 0))
    return call(
        product_body,
        [struct(steps, span, width)] * 4,
        (6 * rows * depth * width, rows * depth * 4 + depth * width * 4),
        grid_spec=pltpu.PrefetchScalarGridSpec(
            num_scalar_prefetch=1,
            grid=(steps,),
            in_specs=[spec, spec, whole, whole],
            out_specs=[pl.BlockSpec((1, span, width), lambda i, where: (i, 0, 0))] * 4,
            scratch_shapes=[
                pltpu.VMEM((depth, width), jnp.bfloat16),
                pltpu.VMEM((depth, width), jnp.bfloat16),
                pltpu.VMEM((NB, width), jnp.float32),
            ],
        ),
    )(where, high, low, near, far)


def smem():
    return pl.BlockSpec(memory_space=pltpu.SMEM)


def vmem():
    return pl.BlockSpec(memory_space=pltpu.VMEM)


def lay_top_body(where, near, planes, far, planes_x, high, low, scratch):
    prow, layer, core = where[0], where[1], where[2]
    blocks = scratch.shape[0]
    rows = planes.shape[2]
    skip = near.shape[1] - rows
    share = rows // (blocks // 2)
    sub = 4 * share
    for side, (same, other) in enumerate(((near, planes), (far, planes_x))):
        for slot in range(NZ):
            for d in range(4):
                at = ((layer ^ slot) * 2 + (core ^ side)) * sub + (prow ^ d) * share
                at = pl.multiple_of(at, share)
                for block in range(blocks):
                    start = (block % (blocks // 2)) * share
                    lanes = slice(block // (blocks // 2) * NB, (block // (blocks // 2) + 1) * NB)
                    if d == 0:
                        first = skip + start
                        value = same[slot, first : first + share, lanes]
                    else:
                        value = other[d - 1, slot, start : start + share, lanes]
                    scratch[block, pl.ds(at, share), :] = value
    for block in range(blocks):
        high[block], low[block] = split(scratch[block])


def lay_top(where, blocks, *arrays):
    shape = struct(blocks, NB, NB, dtype=jnp.bfloat16)
    return call(
        lay_top_body,
        (shape, shape),
        (0, 3 * blocks * NB * NB * 4),
        in_specs=[smem()] + [vmem()] * 4,
        out_specs=[vmem()] * 2,
        scratch_shapes=[pltpu.VMEM((blocks, NB, NB), jnp.float32)],
    )(where, *arrays)


def panel_body(panels, done, parts_in, *refs):
    where, refs = refs[0], refs[1:]
    images, refs = refs[:parts_in], refs[parts_in:]
    adjoint, factor, top_high, top_low, adjoint_top = refs[:5]
    refs = refs[5:]
    lower_in, refs = refs[: len(done)], refs[len(done) :]
    blocks_in, refs = refs[: bool(done)], refs[bool(done) :]
    last = 0 in panels
    if last:
        grad, keep, send, image, scratch = refs
        lower_out = blocks_out = None
    else:
        lower_out, refs = refs[: len(panels)], refs[len(panels) :]
        blocks_out, keep, send, image, scratch = refs
    prow, pcol, core = where[0], where[1], where[2]
    if parts_in == 2:
        same, cross = images
        steps, sub = same.shape[0], same.shape[1]
        for k in range(steps):
            image[pl.ds(pl.multiple_of((2 * k + core) * sub, sub), sub), :] = same[k]
            image[pl.ds(pl.multiple_of((2 * k + 1 - core) * sub, sub), sub), :] = cross[k]
    else:
        image[...] = images[0][...]

    def block(row, column):
        slot = block_slot(row, column)
        return top_high[slot], top_low[slot]

    def block_row(row, columns):
        parts = [block(row, column) for column in range(columns)]
        return tuple(jnp.concatenate([part[i] for part in parts], 1) for i in range(2))

    def inverse(panel):
        slot = block_slot(K, 0) + panel
        return top_high[slot], top_low[slot]

    lower, parts = {}, {}
    for at, panel in enumerate(done):
        lower[panel] = lower_in[at][...]
        parts[panel] = split(lower[panel])
    columns = [split(panel_of(factor, panel)) for panel in range(max(panels) + 1)]
    terms = {}
    for at, panel in enumerate(panels):
        residual = panel_of(adjoint, panel) - 2.0 * image[:, at * NB : (at + 1) * NB]
        for later in range(panel + 1, K):
            residual = residual - dot3(parts[later], block(later, panel))
        value = dot3(split(residual), inverse(panel))
        lower[panel] = value
        parts[panel] = split(value)
        turned = split(value.T)
        for earlier in range(panel + 1):
            terms[panel, earlier] = -dot3(turned, columns[earlier])
    if last:
        for panel in range(K):
            for half in range(2):
                grad[pl.ds(4 * half + panel, grad.shape[0] // 8, stride=8), :] = lower[panel][
                    :, half * LANES : (half + 1) * LANES
                ]
    else:
        for at, panel in enumerate(panels):
            lower_out[at][...] = lower[panel]

    share = adjoint_top.shape[1]
    mine = jnp.where(prow == 0, 1.0, 0.0)
    upper, diag = {}, {}
    if done:
        slots = sorted(block_slot(r, c) for r in done for c in range(r + 1))
        for r in done:
            for c in range(r):
                upper[c, r] = blocks_in[0][slots.index(block_slot(r, c))]
    rows = {}
    for row in panels:
        flipped = {b: split(upper[row, b].T) for b in range(row + 1, K)}
        total = []
        for column in range(row + 1):
            scratch[...] = terms[row, column]
            at = pl.ds(pl.multiple_of(pcol * share, share), share)
            scratch[at, :] = scratch[at, :] + mine * adjoint_top[block_slot(row, column)]
            total.append(scratch[...])
        for b in range(row + 1, K):
            for column in range(row + 1):
                total[column] = total[column] - dot3(flipped[b], block(b, column))
        ids = [lax.broadcasted_iota(jnp.int32, (NB, NB), axis) for axis in range(2)]
        lower_adj = jnp.where(ids[0] >= ids[1], total[row], 0.0)
        d_high, d_low = block(row, row)
        factor_block = d_high.astype(jnp.float32) + d_low.astype(jnp.float32)
        factor_block = jnp.where(ids[0] >= ids[1], factor_block, 0.0).T
        inner = dot3(split(factor_block), split(lower_adj))
        inner = jnp.where(ids[0] > ids[1], inner, jnp.where(ids[0] == ids[1], 0.5 * inner, 0.0))
        i_high, i_low = inverse(row)
        turned = (i_high.astype(jnp.float32) + i_low.astype(jnp.float32)).T
        spread = dot3(split(turned), split(dot3(split(inner), inverse(row))))
        diag[row] = 0.5 * (spread + spread.T)
        doubled = split(2.0 * diag[row])
        for column in range(row):
            total[column] = total[column] - dot3(doubled, block(row, column))
        for column in reversed(range(row)):
            for middle in range(column + 1, row):
                total[column] = total[column] - dot3(split(upper[middle, row]), block(middle, column))
            upper[column, row] = dot3(split(total[column]), inverse(column))
        for column in range(row):
            rows[row, column] = upper[column, row]
        rows[row, row] = diag[row]
    for at, key in enumerate(sorted(rows)):
        scratch[...] = rows[key]
        if blocks_out is not None:
            blocks_out[at] = rows[key]
        for z in range(NZ):
            for target, which in ((keep, core), (send, 1 - core)):
                start = pl.multiple_of(z * 2 * share + which * share, share)
                target[at, z] = scratch[pl.ds(start, share), :]


def panel_group(panels, done, where, images, views, top, adjoint_top, lower, blocks):
    local_rows = views[0].shape[0] // 8
    share = adjoint_top.shape[1]
    count = sum(panel + 1 for panel in panels)
    scattered = [struct(count, NZ, share, NB)] * 2
    if 0 in panels:
        out = [struct(*views[0].shape)] + scattered
    else:
        out = [struct(local_rows, NB)] * len(panels) + [struct(count, NB, NB)] + scattered
    arrays = (where, *images, *views, *top, adjoint_top, *lower, *blocks)
    work = 40 * 6 * NB**3
    return call(
        lambda *refs: panel_body(panels, done, len(images), *refs),
        out,
        (work, 10 * 1024 * 1024),
        in_specs=[smem()] + [vmem()] * (len(arrays) - 1),
        out_specs=[vmem()] * len(out),
        scratch_shapes=[
            pltpu.VMEM((local_rows, len(panels) * NB), jnp.float32),
            pltpu.VMEM((NB, NB), jnp.float32),
        ],
    )(*arrays)


def per_device(adjoint_trail, factor_low, adjoint_low, factor_top, adjoint_top, diag_inverse):
    cycles, sub_rows = factor_low.shape[0], factor_low.shape[3]
    col_cycles = adjoint_trail.shape[3]
    prow, pcol = lax.axis_index("prow"), lax.axis_index("pcol")
    layer, core = pcol // 2, pcol % 2
    holds = jnp.array(HOLDS, jnp.int32)
    shares = factor_top.shape[1]
    count = factor_top.shape[0]
    where = jnp.stack([prow, pcol, core]).astype(jnp.int32)
    quarters = [holds[prow ^ d, layer] for d in range(4)]
    quarters = jnp.stack(quarters + [layer, core]).astype(jnp.int32)
    spot = jnp.stack([prow, layer, core]).astype(jnp.int32)

    views = (eighths(adjoint_low), eighths(factor_low))
    part = shares // 4
    top_all = jnp.concatenate([factor_top, diag_inverse])
    total_blocks = top_all.shape[0]
    extra = pick(top_all.reshape(total_blocks, 4, part, NB), prow, 1)
    extra = extra.reshape(2, total_blocks // 2 * part, NB)
    extra = jnp.concatenate([extra[0], extra[1]], 1)

    rows = cycles * sub_rows
    trail = adjoint_trail.reshape(cycles, 2 * NZ, sub_rows * 8, LANES)

    barrier = lax.optimization_barrier
    mine = take_parts(GROUPS[1], core[None].astype(jnp.int32), views[1], sub_rows)
    mine = [move(mine[s], BACK[s]) for s in (0, 1)]
    own = take(GROUPS[0], views[1], extra)
    line = [own, move(own, LINE[1])]
    halves = halve(trail)
    mine, halves, line = barrier((jnp.stack(mine), halves, line))

    line += [move(own, LINE[2]), move(own, LINE[3])]
    spread = [mine] + [move(mine, PLANE[d]) for d in (1, 2, 3)]
    turned = turn(trail)
    spread, turned, line = barrier((spread, turned, line))

    near = jnp.stack(line)
    leaving = column_product(halves, 1, quarters, spread)
    arriving = move(leaving, CORE)
    far = move(near, CORE)
    staying = column_product(halves, 0, quarters, spread)
    staying, arriving = barrier((staying, arriving))

    term = [staying[d] + arriving[d] for d in range(NZ)]
    came = move(jnp.stack([term[2], term[3]]), MIDDLE_IN)
    extras = near[:, rows:]
    planes = [move(extras, PLANE[d]) for d in (1, 2, 3)]
    outs = product(turned, quarters, near, far)
    outs, planes, came = barrier((outs, planes, came))

    folded = [
        move(term[3] + came[0], MIDDLE_OUT[3]),
        move(term[2] + came[1], MIDDLE_OUT[2]),
        move(term[1], LINE[1]),
    ]
    parts = [move(outs[d], PLANE[d]) for d in (1, 2, 3)]
    planes = jnp.stack(planes)
    top = lay_top(spot, total_blocks, near, planes, far, move(planes, CORE))
    parts, top = barrier((parts, top))

    total = (outs[0] + sum(parts)).reshape(col_cycles, 2, sub_rows, -1)
    same = move(pick(total, layer // 2, 1), HOME[0])
    cross = move(pick(total, 1 - layer // 2, 1), HOME[1])
    same, cross, folded = barrier((same, cross, folded))

    def strips(kept):
        kept = kept.reshape(kept.shape[0], NZ, 4, part, NB)
        strip = pick(kept, prow, 2)
        for d in (1, 2, 3):
            strip = strip + move(pick(kept, prow ^ d, 2), PLANE[d])
        return strip

    *lower, blocks, keep, send = panel_group(
        GROUPS[0], (), where, (same, cross), views, top, adjoint_top, (), ()
    )
    kept = keep + move(send, CORE)
    kept, folded = barrier((kept, folded))
    second_image = term[0] + sum(folded)
    strip = strips(kept)
    low_out, keep, send = panel_group(
        GROUPS[1], GROUPS[0], where, (second_image,), views, top, adjoint_top, lower, (blocks,)
    )
    keep, send, strip = barrier((keep, send, strip))
    strip = jnp.concatenate([strips(keep + move(send, CORE)), strip])
    own_strip = pick(strip, layer, 1)
    for d in (1, 2, 3):
        own_strip = own_strip + move(pick(strip, layer ^ d, 1), LINE[d])
    pieces = [own_strip] + [move(own_strip, PLANE[d]) for d in (1, 2, 3)]
    for bit in (1, 2):
        pieces = [jnp.where(prow & bit, pieces[d ^ bit], pieces[d]) for d in range(4)]
    grad_top = jnp.stack(pieces, 1).reshape(count, 4 * part, NB)
    grad_low = low_out.reshape(rows, 2, K, LANES).transpose(0, 2, 1, 3).reshape(factor_low.shape)
    return (grad_low, grad_top)


def covers(mesh):
    return mesh.shape["prow"] == 4 and mesh.shape["pcol"] == 8


def solution(mesh):
    in_specs = (
        P(None, "prow", None, None, "pcol", None),
        P(None, "prow", "pcol", None, None, None),
        P(None, "prow", "pcol", None, None, None),
        P(None, "pcol", None),
        P(None, "pcol", None),
        P(None, "pcol", None),
    )
    out_specs = (P(None, "prow", "pcol", None, None, None), P(None, "pcol", None))
    return jax.shard_map(
        per_device if covers(mesh) else per_device_any, mesh=mesh, in_specs=in_specs, out_specs=out_specs, check_vma=False
    )
```

```python
import jax
import jax.numpy as jnp
from jax import lax
from jax.experimental import pallas as pl
from jax.experimental.pallas import tpu as pltpu
from jax.sharding import PartitionSpec as P

NB = 256
K = 4


HIGHEST = lax.Precision.HIGHEST


def from_root(array, axis, root):
    mine = lax.axis_index(axis) == root
    return lax.psum(jnp.where(mine, array, jnp.zeros_like(array)), axis)


def matmul(left, right):
    return jnp.dot(left, right, precision=HIGHEST, preferred_element_type=jnp.float32)


def inner_product(left, right):
    return lax.dot_general(
        left, right, (((0,), (0,)), ((), ())), precision=HIGHEST, preferred_element_type=jnp.float32
    )


def block_slot(row_block, col_block):
    return row_block * (row_block + 1) // 2 + col_block


def half_lower(square):
    size = square.shape[0]
    row_ids = lax.broadcasted_iota(jnp.int32, (size, size), 0)
    col_ids = lax.broadcasted_iota(jnp.int32, (size, size), 1)
    return jnp.where(row_ids > col_ids, square, jnp.where(row_ids == col_ids, 0.5 * square, 0.0))


def diagonal_adjoint(diagonal, inverse, lower_adj):
    inner = half_lower(inner_product(jnp.tril(diagonal), lower_adj))
    spread = inner_product(inverse, matmul(inner, inverse))
    return 0.5 * (spread + spread.T)


def rows_one(piece):
    return lax.all_gather(piece, "pcol", axis=1, tiled=True)


def owner_one(piece, root):
    return from_root(piece, "prow", root)


def reduce_one(term, count):
    return lax.psum_scatter(
        term(jnp.int32(0), lax.axis_size("pcol") * count), "pcol", scatter_dimension=0, tiled=True
    )


def trailing_product(trail, panels, gather_rows, send_owner, reduce_rows):
    prow_count = lax.axis_size("prow")
    pcol_count = lax.axis_size("pcol")
    cycles, sub_rows, width = panels.shape
    block = sub_rows * pcol_count
    gathered = gather_rows(panels[:, None]).reshape(cycles, block, width)
    column = lax.axis_index("pcol")
    col_cycles = trail.shape[3]
    owned = []
    for cycle in range(col_cycles):
        global_block = cycle * pcol_count + column
        share = lax.dynamic_index_in_dim(gathered, global_block // prow_count, 0, keepdims=False)
        owned.append(send_owner(share, global_block % prow_count))
    stacked = jnp.stack(owned)
    view = trail.reshape(cycles, pcol_count, sub_rows, col_cycles, block)
    unit = cycles * sub_rows

    def term(start, count):
        product = jnp.einsum(
            "iaekb,kbn->aien", view, stacked, precision=HIGHEST, preferred_element_type=jnp.float32
        )
        return product.reshape(count, width)

    return reduce_rows(term, unit).reshape(cycles, sub_rows, width)


def per_device_any(adjoint_trail, factor_low, adjoint_low, factor_top, adjoint_top, diag_inverse):
    cycles = factor_low.shape[0]
    sub_rows = factor_low.shape[3]
    local_rows = cycles * sub_rows
    low_factor = factor_low.reshape(cycles, sub_rows, K * NB)
    low_adjoint = adjoint_low.reshape(local_rows, K, NB)
    columns = low_factor.reshape(local_rows, K, NB)
    top_factor, top_adjoint, inverses = (
        lax.all_gather(factor_top, "pcol", axis=1, tiled=True),
        lax.all_gather(adjoint_top, "pcol", axis=1, tiled=True),
        lax.all_gather(diag_inverse, "pcol", axis=1, tiled=True),
    )
    lower_grads = [None] * K
    diag_grads = [None] * K
    upper_grads = {}
    grams = {}

    def lower_step(panel):
        single = low_factor[:, :, panel * NB : (panel + 1) * NB]
        image = trailing_product(adjoint_trail, single, rows_one, owner_one, reduce_one).reshape(
            local_rows, NB
        )
        residual = low_adjoint[:, panel] - 2.0 * image
        for later in range(panel + 1, K):
            residual = residual - matmul(lower_grads[later], top_factor[block_slot(later, panel)])
        lower_grads[panel] = matmul(residual, inverses[panel])

    def top_step(panel):
        for row_block in range(panel + 1, K):
            top_residual = top_adjoint[block_slot(row_block, panel)] - grams[row_block, panel]
            top_residual = top_residual - 2.0 * matmul(
                diag_grads[row_block], top_factor[block_slot(row_block, panel)]
            )
            for middle in range(panel + 1, row_block):
                top_residual = top_residual - matmul(
                    upper_grads[middle, row_block], top_factor[block_slot(middle, panel)]
                )
            for beyond in range(row_block + 1, K):
                top_residual = top_residual - inner_product(
                    upper_grads[row_block, beyond], top_factor[block_slot(beyond, panel)]
                )
            upper_grads[panel, row_block] = matmul(top_residual, inverses[panel])
        lower_adj = top_adjoint[block_slot(panel, panel)] - grams[panel, panel]
        for row_block in range(panel + 1, K):
            lower_adj = lower_adj - inner_product(
                upper_grads[panel, row_block], top_factor[block_slot(row_block, panel)]
            )
        diag_grads[panel] = diagonal_adjoint(
            top_factor[block_slot(panel, panel)], inverses[panel], jnp.tril(lower_adj)
        )

    for panel in reversed(range(K)):
        lower_step(panel)
        local_gram = jnp.stack(
            [inner_product(lower_grads[panel], columns[:, earlier]) for earlier in range(panel + 1)]
        )
        summed = lax.psum(local_gram, ("prow", "pcol"))
        for earlier in range(panel + 1):
            grams[panel, earlier] = summed[earlier]
        top_step(panel)
    grad_low = jnp.stack(lower_grads, 1).reshape(factor_low.shape)
    blocks = []
    for row_block in range(K):
        for col_block in range(row_block + 1):
            if row_block == col_block:
                blocks.append(diag_grads[col_block])
            else:
                blocks.append(upper_grads[col_block, row_block])
    full_top = jnp.stack(blocks)
    share_rows = factor_top.shape[1]
    grad_top = lax.dynamic_slice_in_dim(
        full_top, lax.axis_index("pcol") * share_rows, share_rows, 1
    )
    return (grad_low, grad_top)


AXES = ("prow", "pcol")
NZ = 4
LANES = 128
VMEM = 48 * 1024 * 1024
GROUPS = ((3, 2), (1, 0))
HOLDS = ((0, 2, 1, 3), (1, 3, 0, 2), (2, 0, 3, 1), (3, 1, 2, 0))


def route(place):
    pairs = []
    for prow in range(4):
        for pcol in range(8):
            goal = place(prow, pcol // 2, pcol % 2)
            if goal is not None:
                pairs.append((prow * 8 + pcol, goal[0] * 8 + goal[1] * 2 + goal[2]))
    return pairs


CORE = route(lambda p, z, c: (p, z, 1 - c))
PLANE = {d: route(lambda p, z, c, d=d: (p ^ d, z, c)) for d in (1, 2, 3)}
LINE = {d: route(lambda p, z, c, d=d: (p, z ^ d, c)) for d in (1, 2, 3)}
MIDDLE_IN = route(lambda p, z, c: (p, z ^ 1, c) if z in (0, 3) else None)
MIDDLE_OUT = {d: route(lambda p, z, c, d=d: (p, z ^ d, c) if z in (1, 2) else None) for d in (2, 3)}
HOME = {
    s: route(lambda p, z, c, s=s: ((z % 2) * 2 + c, HOLDS[p][z], (z // 2) ^ s)) for s in (0, 1)
}

BACK = {s: [(goal, source) for source, goal in HOME[s]] for s in (0, 1)}


def move(array, pairs):
    return lax.ppermute(array, AXES, pairs)


def pick(array, index, axis):
    return lax.dynamic_index_in_dim(array, index, axis, keepdims=False)


def call(body, out, cost, **more):
    flops, bytes_accessed = cost
    return pl.pallas_call(
        body,
        out_shape=out,
        compiler_params=pltpu.CompilerParams(vmem_limit_bytes=VMEM),
        cost_estimate=pl.CostEstimate(
            flops=flops, bytes_accessed=bytes_accessed, transcendentals=0
        ),
        **more,
    )


def struct(*shape, dtype=jnp.float32):
    return jax.ShapeDtypeStruct(shape, dtype)


def split(value):
    high = value.astype(jnp.bfloat16)
    return high, (value - high.astype(jnp.float32)).astype(jnp.bfloat16)


def dot(left, right):
    return jnp.dot(left, right, preferred_element_type=jnp.float32)


def dot3(left, right):
    return dot(left[0], right[0]) + (dot(left[0], right[1]) + dot(left[1], right[0]))


def panel_of(view, panel):
    rows = view.shape[0] // 8
    halves = [view[pl.ds(4 * half + panel, rows, stride=8), :] for half in range(2)]
    return jnp.concatenate(halves, 1)


def eighths(array):
    rows = array.size // (K * NB)
    return array.reshape(rows, K, 2, LANES).transpose(0, 2, 1, 3).reshape(rows * 8, LANES)


def take_body(panels, view, extra, out):
    rows = view.shape[0] // 8
    for at, panel in enumerate(panels):
        out[:rows, at * NB : (at + 1) * NB] = panel_of(view, panel)
    if extra is not None:
        out[rows:, :] = extra[...]


def take(panels, view, extra):
    rows = view.shape[0] // 8
    width = len(panels) * NB
    if extra is None:
        return call(
            lambda v, o: take_body(panels, v, None, o), struct(rows, width), (0, 2 * view.size)
        )(view)
    return call(
        lambda v, e, o: take_body(panels, v, e, o),
        struct(rows + extra.shape[0], width),
        (0, 2 * view.size),
    )(view, extra)


def take_parts_body(panels, core, view, same, cross, scratch):
    steps, sub = same.shape[0], same.shape[1]
    for at, panel in enumerate(panels):
        scratch[:, at * NB : (at + 1) * NB] = panel_of(view, panel)
    for k in range(steps):
        for out, odd in ((same, core[0]), (cross, 1 - core[0])):
            out[k] = scratch[pl.ds(pl.multiple_of((2 * k + odd) * sub, sub), sub), :]


def take_parts(panels, core, view, sub):
    rows, width = view.shape[0] // 8, len(panels) * NB
    shape = struct(rows // sub // 2, sub, width)
    return call(
        lambda *refs: take_parts_body(panels, *refs),
        [shape, shape],
        (0, 2 * view.size),
        in_specs=[smem(), vmem()],
        out_specs=[vmem(), vmem()],
        scratch_shapes=[pltpu.VMEM((rows, width), jnp.float32)],
    )(core, view)


def halve_body(block, high, low):
    rows = block.shape[0] * block.shape[2] // 8
    flat = block.reshape(rows * 8, LANES)
    for part in range(8):
        lanes = slice(part * LANES, (part + 1) * LANES)
        high[0, :, lanes], low[0, :, lanes] = split(flat[pl.ds(part, rows, stride=8), :])


def halve(trail):
    cycles, slots, rows, _ = trail.shape
    unit = cycles * rows // 8
    spec = pl.BlockSpec((1, unit, 8 * LANES), lambda i: (i, 0, 0))
    shape = struct(slots, unit, 8 * LANES, dtype=jnp.bfloat16)
    return call(
        halve_body,
        (shape, shape),
        (0, 2 * trail.size * 4),
        grid=(slots,),
        in_specs=[pl.BlockSpec((cycles, 1, rows, LANES), lambda i: (0, i, 0, 0))],
        out_specs=[spec, spec],
    )(trail)


def column_body(where, high, low, *refs):
    quarters, out, c_high, c_low = refs[:4], refs[4], refs[5], refs[6]

    @pl.when(pl.program_id(0) == 0)
    def _():
        for d in range(4):
            for side in range(2):
                source = quarters[d]
                sub = source.shape[2]
                for k in range(source.shape[1]):
                    at = k * NB + (where[d] * 2 + ((where[4] // 2) ^ side)) * sub
                    at = pl.ds(pl.multiple_of(at, sub), sub)
                    c_high[at, :], c_low[at, :] = split(source[side, k])

    out[0] = dot3((high[0], low[0]), (c_high[...], c_low[...]))


def column_again_body(where, high, low, c_high, c_low, out):
    out[0] = dot3((high[0], low[0]), (c_high[...], c_low[...]))


def column_product(halves, side, where, quarters, split_rows=None):
    unit, depth = halves[0].shape[1:]
    width = quarters[0].shape[3]

    def slot(i, where):
        return ((where[4] ^ i) * 2 + (where[5] ^ side), 0, 0)

    rows_spec = pl.BlockSpec((depth, width), lambda i, where: (0, 0))
    out_spec = pl.BlockSpec((1, unit, width), lambda i, where: (i, 0, 0))
    out_shape = struct(NZ, unit, width)
    cost = (6 * NZ * unit * depth * width, NZ * unit * depth * 4 + depth * width * 4)
    given = quarters if split_rows is None else split_rows
    if split_rows is None:
        specs = [pl.BlockSpec(q.shape, lambda i, where: (0, 0, 0, 0)) for q in quarters]
        out_spec = [out_spec, rows_spec, rows_spec]
        out_shape = [out_shape] + [struct(depth, width, dtype=jnp.bfloat16)] * 2
    else:
        specs = [rows_spec, rows_spec]
    return call(
        column_body if split_rows is None else column_again_body,
        out_shape,
        cost,
        grid_spec=pltpu.PrefetchScalarGridSpec(
            num_scalar_prefetch=1,
            grid=(NZ,),
            in_specs=[pl.BlockSpec((1, unit, depth), slot)] * 2 + specs,
            out_specs=out_spec,
        ),
    )(where, *halves, *given)


def turn_body(block, high, low):
    rows = block.shape[0] * block.shape[2] // 8
    flat = block.reshape(rows * 8, LANES)
    for part in range(8):
        value = flat[pl.ds(part, rows, stride=8), :].T
        top, rest = split(value)
        high[part * LANES : (part + 1) * LANES, :] = top
        low[part * LANES : (part + 1) * LANES, :] = rest


def turn(trail):
    cycles, slots, rows, _ = trail.shape
    unit = cycles * rows // 8
    spec = pl.BlockSpec((8 * LANES, unit), lambda i: (0, i))
    shape = struct(8 * LANES, slots * unit, dtype=jnp.bfloat16)
    return call(
        turn_body,
        (shape, shape),
        (0, 2 * trail.size * 4),
        grid=(slots,),
        in_specs=[pl.BlockSpec((cycles, 1, rows, LANES), lambda i: (0, i, 0, 0))],
        out_specs=[spec, spec],
    )(trail)


def product_body(where, high, low, near, far, *rest):
    outs, (c_high, c_low, total) = rest[:4], rest[4:]
    unit = high.shape[1] // (2 * NZ)

    @pl.when(pl.program_id(0) == 0)
    def _():
        for side, source in enumerate((near, far)):
            for d in range(NZ):
                at = ((where[4] ^ d) * 2 + (where[5] ^ side)) * unit
                at = pl.ds(pl.multiple_of(at, unit), unit)
                c_high[at, :], c_low[at, :] = split(source[d, :unit, :])

    total[...] = dot3((high[...], low[...]), (c_high[...], c_low[...]))
    span = total.shape[0] // NZ
    for d in range(4):
        outs[d][0] = total[pl.ds(pl.multiple_of(where[d] * span, span), span), :]


def product(turned, where, near, far):
    high, low = turned
    rows, depth = high.shape
    width = near.shape[2]
    steps = rows // NB
    span = NB // NZ
    spec = pl.BlockSpec((NB, depth), lambda i, where: (i, 0))
    whole = pl.BlockSpec(near.shape, lambda i, where: (0, 0, 0))
    return call(
        product_body,
        [struct(steps, span, width)] * 4,
        (6 * rows * depth * width, rows * depth * 4 + depth * width * 4),
        grid_spec=pltpu.PrefetchScalarGridSpec(
            num_scalar_prefetch=1,
            grid=(steps,),
            in_specs=[spec, spec, whole, whole],
            out_specs=[pl.BlockSpec((1, span, width), lambda i, where: (i, 0, 0))] * 4,
            scratch_shapes=[
                pltpu.VMEM((depth, width), jnp.bfloat16),
                pltpu.VMEM((depth, width), jnp.bfloat16),
                pltpu.VMEM((NB, width), jnp.float32),
            ],
        ),
    )(where, high, low, near, far)


def smem():
    return pl.BlockSpec(memory_space=pltpu.SMEM)


def vmem():
    return pl.BlockSpec(memory_space=pltpu.VMEM)


def lay_top_body(where, near, planes, far, planes_x, high, low, scratch):
    prow, layer, core = where[0], where[1], where[2]
    blocks = scratch.shape[0]
    rows = planes.shape[2]
    skip = near.shape[1] - rows
    share = rows // (blocks // 2)
    sub = 4 * share
    for side, (same, other) in enumerate(((near, planes), (far, planes_x))):
        for slot in range(NZ):
            for d in range(4):
                at = ((layer ^ slot) * 2 + (core ^ side)) * sub + (prow ^ d) * share
                at = pl.multiple_of(at, share)
                for block in range(blocks):
                    start = (block % (blocks // 2)) * share
                    lanes = slice(block // (blocks // 2) * NB, (block // (blocks // 2) + 1) * NB)
                    if d == 0:
                        first = skip + start
                        value = same[slot, first : first + share, lanes]
                    else:
                        value = other[d - 1, slot, start : start + share, lanes]
                    scratch[block, pl.ds(at, share), :] = value
    for block in range(blocks):
        high[block], low[block] = split(scratch[block])


def lay_top(where, blocks, *arrays):
    shape = struct(blocks, NB, NB, dtype=jnp.bfloat16)
    return call(
        lay_top_body,
        (shape, shape),
        (0, 3 * blocks * NB * NB * 4),
        in_specs=[smem()] + [vmem()] * 4,
        out_specs=[vmem()] * 2,
        scratch_shapes=[pltpu.VMEM((blocks, NB, NB), jnp.float32)],
    )(where, *arrays)


def panel_body(panels, done, parts_in, *refs):
    where, refs = refs[0], refs[1:]
    images, refs = refs[:parts_in], refs[parts_in:]
    adjoint, factor, top_high, top_low, adjoint_top = refs[:5]
    refs = refs[5:]
    lower_in, refs = refs[: len(done)], refs[len(done) :]
    blocks_in, refs = refs[: bool(done)], refs[bool(done) :]
    last = 0 in panels
    if last:
        grad, keep, send, image, scratch = refs
        lower_out = blocks_out = None
    else:
        lower_out, refs = refs[: len(panels)], refs[len(panels) :]
        blocks_out, keep, send, image, scratch = refs
    prow, pcol, core = where[0], where[1], where[2]
    if parts_in == 2:
        same, cross = images
        steps, sub = same.shape[0], same.shape[1]
        for k in range(steps):
            image[pl.ds(pl.multiple_of((2 * k + core) * sub, sub), sub), :] = same[k]
            image[pl.ds(pl.multiple_of((2 * k + 1 - core) * sub, sub), sub), :] = cross[k]
    else:
        image[...] = images[0][...]

    def block(row, column):
        slot = block_slot(row, column)
        return top_high[slot], top_low[slot]

    def block_row(row, columns):
        parts = [block(row, column) for column in range(columns)]
        return tuple(jnp.concatenate([part[i] for part in parts], 1) for i in range(2))

    def inverse(panel):
        slot = block_slot(K, 0) + panel
        return top_high[slot], top_low[slot]

    lower, parts = {}, {}
    for at, panel in enumerate(done):
        lower[panel] = lower_in[at][...]
        parts[panel] = split(lower[panel])
    columns = [split(panel_of(factor, panel)) for panel in range(max(panels) + 1)]
    terms = {}
    for at, panel in enumerate(panels):
        residual = panel_of(adjoint, panel) - 2.0 * image[:, at * NB : (at + 1) * NB]
        for later in range(panel + 1, K):
            residual = residual - dot3(parts[later], block(later, panel))
        value = dot3(split(residual), inverse(panel))
        lower[panel] = value
        parts[panel] = split(value)
        turned = split(value.T)
        for earlier in range(panel + 1):
            terms[panel, earlier] = -dot3(turned, columns[earlier])
    if last:
        for panel in range(K):
            for half in range(2):
                grad[pl.ds(4 * half + panel, grad.shape[0] // 8, stride=8), :] = lower[panel][
                    :, half * LANES : (half + 1) * LANES
                ]
    else:
        for at, panel in enumerate(panels):
            lower_out[at][...] = lower[panel]

    share = adjoint_top.shape[1]
    mine = jnp.where(prow == 0, 1.0, 0.0)
    upper, diag = {}, {}
    if done:
        slots = sorted(block_slot(r, c) for r in done for c in range(r + 1))
        for r in done:
            for c in range(r):
                upper[c, r] = blocks_in[0][slots.index(block_slot(r, c))]
    rows = {}
    for row in panels:
        flipped = {b: split(upper[row, b].T) for b in range(row + 1, K)}
        total = []
        for column in range(row + 1):
            scratch[...] = terms[row, column]
            at = pl.ds(pl.multiple_of(pcol * share, share), share)
            scratch[at, :] = scratch[at, :] + mine * adjoint_top[block_slot(row, column)]
            total.append(scratch[...])
        for b in range(row + 1, K):
            for column in range(row + 1):
                total[column] = total[column] - dot3(flipped[b], block(b, column))
        ids = [lax.broadcasted_iota(jnp.int32, (NB, NB), axis) for axis in range(2)]
        lower_adj = jnp.where(ids[0] >= ids[1], total[row], 0.0)
        d_high, d_low = block(row, row)
        factor_block = d_high.astype(jnp.float32) + d_low.astype(jnp.float32)
        factor_block = jnp.where(ids[0] >= ids[1], factor_block, 0.0).T
        inner = dot3(split(factor_block), split(lower_adj))
        inner = jnp.where(ids[0] > ids[1], inner, jnp.where(ids[0] == ids[1], 0.5 * inner, 0.0))
        i_high, i_low = inverse(row)
        turned = (i_high.astype(jnp.float32) + i_low.astype(jnp.float32)).T
        spread = dot3(split(turned), split(dot3(split(inner), inverse(row))))
        diag[row] = 0.5 * (spread + spread.T)
        doubled = split(2.0 * diag[row])
        for column in range(row):
            total[column] = total[column] - dot3(doubled, block(row, column))
        for column in reversed(range(row)):
            for middle in range(column + 1, row):
                total[column] = total[column] - dot3(split(upper[middle, row]), block(middle, column))
            upper[column, row] = dot3(split(total[column]), inverse(column))
        for column in range(row):
            rows[row, column] = upper[column, row]
        rows[row, row] = diag[row]
    for at, key in enumerate(sorted(rows)):
        scratch[...] = rows[key]
        if blocks_out is not None:
            blocks_out[at] = rows[key]
        for z in range(NZ):
            for target, which in ((keep, core), (send, 1 - core)):
                start = pl.multiple_of(z * 2 * share + which * share, share)
                target[at, z] = scratch[pl.ds(start, share), :]


def panel_group(panels, done, where, images, views, top, adjoint_top, lower, blocks):
    local_rows = views[0].shape[0] // 8
    share = adjoint_top.shape[1]
    count = sum(panel + 1 for panel in panels)
    scattered = [struct(count, NZ, share, NB)] * 2
    if 0 in panels:
        out = [struct(*views[0].shape)] + scattered
    else:
        out = [struct(local_rows, NB)] * len(panels) + [struct(count, NB, NB)] + scattered
    arrays = (where, *images, *views, *top, adjoint_top, *lower, *blocks)
    work = 40 * 6 * NB**3
    return call(
        lambda *refs: panel_body(panels, done, len(images), *refs),
        out,
        (work, 10 * 1024 * 1024),
        in_specs=[smem()] + [vmem()] * (len(arrays) - 1),
        out_specs=[vmem()] * len(out),
        scratch_shapes=[
            pltpu.VMEM((local_rows, len(panels) * NB), jnp.float32),
            pltpu.VMEM((NB, NB), jnp.float32),
        ],
    )(*arrays)


def per_device(adjoint_trail, factor_low, adjoint_low, factor_top, adjoint_top, diag_inverse):
    cycles, sub_rows = factor_low.shape[0], factor_low.shape[3]
    col_cycles = adjoint_trail.shape[3]
    prow, pcol = lax.axis_index("prow"), lax.axis_index("pcol")
    layer, core = pcol // 2, pcol % 2
    holds = jnp.array(HOLDS, jnp.int32)
    shares = factor_top.shape[1]
    count = factor_top.shape[0]
    where = jnp.stack([prow, pcol, core]).astype(jnp.int32)
    quarters = [holds[prow ^ d, layer] for d in range(4)]
    quarters = jnp.stack(quarters + [layer, core]).astype(jnp.int32)
    spot = jnp.stack([prow, layer, core]).astype(jnp.int32)

    views = (eighths(adjoint_low), eighths(factor_low))
    part = shares // 4
    top_all = jnp.concatenate([factor_top, diag_inverse])
    total_blocks = top_all.shape[0]
    extra = pick(top_all.reshape(total_blocks, 4, part, NB), prow, 1)
    extra = extra.reshape(2, total_blocks // 2 * part, NB)
    extra = jnp.concatenate([extra[0], extra[1]], 1)

    rows = cycles * sub_rows
    trail = adjoint_trail.reshape(cycles, 2 * NZ, sub_rows * 8, LANES)

    barrier = lax.optimization_barrier
    mine = take_parts(GROUPS[1], core[None].astype(jnp.int32), views[1], sub_rows)
    mine = [move(mine[s], BACK[s]) for s in (0, 1)]
    own = take(GROUPS[0], views[1], extra)
    line = [own, move(own, LINE[1])]
    halves = halve(trail)
    mine, halves, line = barrier((jnp.stack(mine), halves, line))

    line += [move(own, LINE[2]), move(own, LINE[3])]
    spread = [mine] + [move(mine, PLANE[d]) for d in (1, 2, 3)]
    turned = turn(trail)
    spread, turned, line = barrier((spread, turned, line))

    near = jnp.stack(line)
    leaving, *split_rows = column_product(halves, 1, quarters, spread)
    arriving = move(leaving, CORE)
    far = move(near, CORE)
    staying = column_product(halves, 0, quarters, spread, split_rows)
    staying, arriving = barrier((staying, arriving))

    term = [staying[d] + arriving[d] for d in range(NZ)]
    came = move(jnp.stack([term[2], term[3]]), MIDDLE_IN)
    extras = near[:, rows:]
    planes = [move(extras, PLANE[d]) for d in (1, 2, 3)]
    outs = product(turned, quarters, near, far)
    outs, planes, came = barrier((outs, planes, came))

    folded = [
        move(term[3] + came[0], MIDDLE_OUT[3]),
        move(term[2] + came[1], MIDDLE_OUT[2]),
        move(term[1], LINE[1]),
    ]
    parts = [move(outs[d], PLANE[d]) for d in (1, 2, 3)]
    planes = jnp.stack(planes)
    top = lay_top(spot, total_blocks, near, planes, far, move(planes, CORE))
    parts, top = barrier((parts, top))

    total = (outs[0] + sum(parts)).reshape(col_cycles, 2, sub_rows, -1)
    same = move(pick(total, layer // 2, 1), HOME[0])
    cross = move(pick(total, 1 - layer // 2, 1), HOME[1])
    same, cross, folded = barrier((same, cross, folded))

    def strips(kept):
        kept = kept.reshape(kept.shape[0], NZ, 4, part, NB)
        strip = pick(kept, prow, 2)
        for d in (1, 2, 3):
            strip = strip + move(pick(kept, prow ^ d, 2), PLANE[d])
        return strip

    *lower, blocks, keep, send = panel_group(
        GROUPS[0], (), where, (same, cross), views, top, adjoint_top, (), ()
    )
    kept = keep + move(send, CORE)
    second_image = term[0] + sum(folded)
    strip = strips(kept)
    low_out, keep, send = panel_group(
        GROUPS[1], GROUPS[0], where, (second_image,), views, top, adjoint_top, lower, (blocks,)
    )
    keep, send, strip = barrier((keep, send, strip))
    strip = jnp.concatenate([strips(keep + move(send, CORE)), strip])
    own_strip = pick(strip, layer, 1)
    for d in (1, 2, 3):
        own_strip = own_strip + move(pick(strip, layer ^ d, 1), LINE[d])
    pieces = [own_strip] + [move(own_strip, PLANE[d]) for d in (1, 2, 3)]
    for bit in (1, 2):
        pieces = [jnp.where(prow & bit, pieces[d ^ bit], pieces[d]) for d in range(4)]
    grad_top = jnp.stack(pieces, 1).reshape(count, 4 * part, NB)
    grad_low = low_out.reshape(rows, 2, K, LANES).transpose(0, 2, 1, 3).reshape(factor_low.shape)
    return (grad_low, grad_top)


def covers(mesh):
    return mesh.shape["prow"] == 4 and mesh.shape["pcol"] == 8


def solution(mesh):
    in_specs = (
        P(None, "prow", None, None, "pcol", None),
        P(None, "prow", "pcol", None, None, None),
        P(None, "prow", "pcol", None, None, None),
        P(None, "pcol", None),
        P(None, "pcol", None),
        P(None, "pcol", None),
    )
    out_specs = (P(None, "prow", "pcol", None, None, None), P(None, "pcol", None))
    return jax.shard_map(
        per_device if covers(mesh) else per_device_any, mesh=mesh, in_specs=in_specs, out_specs=out_specs, check_vma=False
    )
```
